512 devices in a mesh: lat: 16 (over z, core), lon: 32 (over y, x).
Axes of the slice: x: 4, y: 8, z: 8, core: 2. Of those that a mesh axis runs over, the one named last changes fastest.
Arguments:
- mlp_input: bfloat16 [512, 384, 640], P('lat', 'lon'), may hold values from -6 to 6
- out_cot: bfloat16 [512, 384, 640], P('lat', 'lon'), may hold values from -6 to 6
- w_in: bfloat16 [640, 1280], replicated, may hold values from -0.25 to 0.25
- w_out: bfloat16 [1280, 640], replicated, may hold values from -0.15625 to 0.15625
- chan_weights: float32 [9, 640], replicated, may hold values from -2 to 2
- row_weights: float32 [9, 512, 9], replicated, may hold values from -2 to 2
- basis_spectra: float32 [9, 384], replicated, may hold values from -6 to 6
- band_cols: int32 [512, 9], replicated, may hold values from 0 to 511, as said below
- band_widths: int32 [512], replicated, may hold values from 1 to 9, as said below
Outputs:
- grid_grad: bfloat16 [512, 384, 640], P('lat', 'lon')
- grad_in: float32 [640, 1280], P('lat', 'lon')
- grad_out: float32 [1280, 640], P('lon', 'lat')
The draws below stay inside these ranges and needn't reach their ends.
Inputs may be any that keep to these rules, and one draw needn't show every extreme that they name: `band_cols`: slot 0 of each row is the row itself; every slot lies within 4 rows of its own row. `band_widths`: the 4 rows nearest each pole use all 9 slots; slots at or beyond a row's width are padding.
All inputs are finite; a program needn't handle non-finite values.
Results may differ from the reference program's by a relative error of at most 0.02.
Values may be sent and summed in bfloat16 or wider, within the bound.
No kernel may reach another device: no remote copies, remote signals or barrier semaphores. Data moves between devices by JAX's collectives and lax.ppermute only.
A program may use at most 64 MiB of HBM per device.

```python
import math
import jax
import jax.numpy as jnp
from jax import lax

C = 640
HID = 1280
NLON = 384
NBASIS = 9
H = 4
LAT_DEV = 32
BAND = 9
NF = 192
LON_DEV = 12
NLAT = 512
N_LAT = 16
N_LON = 32


def draw_band_cols(key, part):
    own_key = jax.random.fold_in(key, 11)
    offsets = jax.random.randint(own_key, (NLAT, BAND), -H, H + 1)
    row_ids = jnp.arange(NLAT, dtype=jnp.int32)[:, None]
    picked = jnp.clip(row_ids + offsets, 0, NLAT - 1)
    picked = picked.at[:, 0].set(row_ids[:, 0])
    return picked.astype(jnp.int32)


def draw_band_widths(key, part):
    own_key = jax.random.fold_in(key, 23)
    drawn = jax.random.randint(own_key, (NLAT,), 1, BAND + 1)
    row_ids = jnp.arange(NLAT, dtype=jnp.int32)
    polar = (row_ids < H) | (row_ids >= NLAT - H)
    return jnp.where(polar, BAND, drawn).astype(jnp.int32)


def level_of(stream_key, dims, cuts, least, high):
    factor_of, own = 1.0, jax.random.fold_in(stream_key, 6)
    for axis_at, blocks in cuts:
        steps = jnp.exp(jax.random.uniform(jax.random.fold_in(own, axis_at), (blocks,), jnp.float32, least / len(cuts), high / len(cuts)))
        factor_of = factor_of * jnp.repeat(steps, dims[axis_at] // blocks).reshape([-1 if axis == axis_at else 1 for axis in range(len(dims))])
    return factor_of


def bell_draw(stream_key, extent, spread, reach, pieces=(), held_as=jnp.bfloat16):
    values = spread * jax.random.normal(stream_key, extent, jnp.float32)
    if pieces:
        values = values * level_of(stream_key, extent, pieces, -0.22, 0.18)
    return jnp.clip(values, -reach, reach).astype(held_as)


def setup_inputs(seed: int = 0) -> dict:
    key_of = jax.random.split(jax.random.key(seed), 10)
    return {
        "mlp_input": bell_draw(key_of[0], (NLAT, NLON, C), 1.0, 6.0, ((0, 16), (1, 32))),
        "out_cot": bell_draw(key_of[1], (NLAT, NLON, C), 1.0, 6.0, ((0, 16), (1, 32))),
        "w_in": bell_draw(key_of[2], (C, HID), C ** -0.5, 0.25),
        "w_out": bell_draw(key_of[3], (HID, C), HID ** -0.5, 0.15625),
        "chan_weights": bell_draw(key_of[4], (NBASIS, C), NBASIS ** -0.5, 2.0, (), jnp.float32),
        "row_weights": bell_draw(key_of[5], (NBASIS, NLAT, BAND), BAND ** -0.5, 2.0, (), jnp.float32),
        "basis_spectra": bell_draw(key_of[6], (NBASIS, 2 * NF), 1.0, 6.0, (), jnp.float32),
        "band_cols": draw_band_cols(jax.random.fold_in(key_of[9], 71), 0),
        "band_widths": draw_band_widths(jax.random.fold_in(key_of[9], 71), 0),
    }


def gelu_parts(pre_act):
    inner_arg = 0.7978845608 * (pre_act + 0.044715 * pre_act * pre_act * pre_act)
    tangent = jnp.tanh(inner_arg)
    gelu_value = 0.5 * pre_act * (1.0 + tangent)
    gelu_slope = 0.5 * (1.0 + tangent) + 0.5 * pre_act * (1.0 - tangent * tangent) * 0.7978845608 * (1.0 + 0.134145 * pre_act * pre_act)
    return gelu_value, gelu_slope


def tables(lon_total):
    half_len = lon_total // 2
    lon_index = jnp.arange(lon_total, dtype=jnp.int32)
    frequency = jnp.arange(2 * half_len, dtype=jnp.int32) % half_len
    phases = (lon_index[:, None] * frequency[None, :]) % lon_total
    angles = phases.astype(jnp.float32) * jnp.float32(2.0 * math.pi / lon_total)
    is_sine = jnp.arange(2 * half_len, dtype=jnp.int32) >= half_len
    forward = jnp.where(is_sine[None, :], jnp.sin(angles), jnp.cos(angles))
    scaling = jnp.where(frequency == 0, jnp.float32(1.0), jnp.float32(2.0)) / jnp.float32(lon_total)
    inverse = forward.T * scaling[:, None]
    return forward, inverse


def weighted(spectra, basis_spectra, chan_w):
    half_len = spectra.shape[-1] // 2
    real_part = spectra[..., :half_len]
    imag_part = spectra[..., half_len:]
    cosine = basis_spectra[:, None, None, :half_len]
    sine = basis_spectra[:, None, None, half_len:]
    first = cosine * real_part[None] + sine * imag_part[None]
    second = cosine * imag_part[None] - sine * real_part[None]
    return jnp.concatenate([first, second], -1) * chan_w[:, None, :, None]


def reference(mlp_input, out_cot, w_in, w_out, chan_weights, row_weights, basis_spectra, band_cols, band_widths):
    lat_total, lon_total, channels = mlp_input.shape
    block_count = N_LAT * N_LON

    def to_blocks(tensor):
        return tensor.reshape(N_LAT, LAT_DEV, N_LON, LON_DEV, channels).transpose(0, 2, 1, 3, 4).reshape(block_count, LAT_DEV * LON_DEV, channels)

    win_f = w_in.astype(jnp.float32)
    wout_f = w_out.astype(jnp.float32)

    def block_step(running, block_pair):
        tokens, cotangent = block_pair
        tok_f = tokens.astype(jnp.float32)
        cot_f = cotangent.astype(jnp.float32)
        pre_act = jnp.dot(tok_f, win_f, preferred_element_type=jnp.float32)
        gelu_value, gelu_slope = gelu_parts(pre_act)
        hidden = gelu_value.astype(jnp.bfloat16)
        back_proj = jnp.dot(cot_f, wout_f.T, preferred_element_type=jnp.float32)
        pre_grad = (back_proj * gelu_slope).astype(jnp.bfloat16)
        grid_cot = (cot_f + jnp.dot(pre_grad.astype(jnp.float32), win_f.T, preferred_element_type=jnp.float32)).astype(jnp.bfloat16)
        part_in = jnp.dot(tok_f.T, pre_grad.astype(jnp.float32), preferred_element_type=jnp.float32)
        part_out = jnp.dot(hidden.astype(jnp.float32).T, cot_f, preferred_element_type=jnp.float32)
        part_in = lax.optimization_barrier(part_in.astype(jnp.bfloat16)).astype(jnp.float32)
        part_out = lax.optimization_barrier(part_out.astype(jnp.bfloat16)).astype(jnp.float32)
        return (running[0] + part_in, running[1] + part_out), grid_cot

    start_sums = (jnp.zeros((channels, HID), jnp.float32), jnp.zeros((HID, channels), jnp.float32))
    (grad_in, grad_out), cot_blocks = lax.scan(block_step, start_sums, (to_blocks(mlp_input), to_blocks(out_cot)))
    grid_cot = cot_blocks.reshape(N_LAT, N_LON, LAT_DEV, LON_DEV, channels).transpose(0, 2, 1, 3, 4).reshape(lat_total, lon_total, channels)

    forward, inverse = tables(lon_total)
    spectra = jnp.einsum("rlc,lg->rcg", grid_cot.astype(jnp.float32), forward, precision=lax.Precision.HIGHEST)
    slot_index = jnp.arange(BAND, dtype=jnp.int32)
    live_mask = (slot_index[None, :] < band_widths[:, None]).astype(jnp.float32)
    coeffs = row_weights * live_mask[None]

    def add_basis(basis, running):
        basis_term = weighted(spectra, lax.dynamic_slice_in_dim(basis_spectra, basis, 1, 0), lax.dynamic_slice_in_dim(chan_weights, basis, 1, 0))[0]
        coeff_rows = lax.dynamic_slice_in_dim(coeffs, basis, 1, 0)[0]
        for slot_pos in range(BAND):
            running = running.at[band_cols[:, slot_pos]].add(coeff_rows[:, slot_pos][:, None, None] * basis_term)
        return running

    filtered = lax.fori_loop(0, NBASIS, add_basis, jnp.zeros(spectra.shape, jnp.float32))
    backed = jnp.einsum("tcg,gl->tlc", filtered, inverse, precision=lax.Precision.HIGHEST).astype(jnp.bfloat16)
    grid_grad = (out_cot.astype(jnp.float32) + backed.astype(jnp.float32)).astype(jnp.bfloat16)
    return (grid_grad, grad_in, grad_out)
```

```python
import functools
import math

import jax
import jax.numpy as jnp
import numpy as np
from jax import lax
from jax.experimental import pallas as pl
from jax.experimental.pallas import tpu as pltpu
from jax.sharding import Mesh, PartitionSpec as P

f32 = jnp.float32
bf16 = jnp.bfloat16
LAT = ("z", "core")
LON = ("y", "x")
ROWS = 32
LONS = 12
PEERS = 32
LOCAL = 20
NLON = 384
NF = 192
NB = 9
REACH = 4
GROUPS = 5
SLAB = LONS * GROUPS
PAD = 64
TALL = PEERS * SLAB + 8


def nt(a, b, precision=None):
    return lax.dot_general(a, b, (((1,), (1,)), ((), ())), preferred_element_type=f32, precision=precision)


def tn(a, b):
    return lax.dot_general(a, b, (((0,), (0,)), ((), ())), preferred_element_type=f32)


def nn(a, b, precision=None):
    return lax.dot_general(a, b, (((1,), (0,)), ((), ())), preferred_element_type=f32, precision=precision)


def swap_quarters(tiles):
    quarter = lax.broadcasted_iota(jnp.int32, tiles[0].shape, 1) // 32
    out = []
    for b in range(4):
        made = None
        for q in range(4):
            shift = (32 * (q - b)) % 128
            moved = pltpu.roll(tiles[q], shift, 1) if shift else tiles[q]
            made = moved if made is None else jnp.where(quarter == q, moved, made)
        out.append(made)
    return out


def gelu_parts(v):
    square = v * v
    tangent = jnp.tanh(0.7978845608 * (v + 0.044715 * v * square))
    half = 0.5 * (1.0 + tangent)
    slope = half + 0.5 * v * (1.0 - tangent * tangent) * 0.7978845608 * (1.0 + 0.134145 * square)
    return v * half, slope


def to_slabs(tall, out):
    for d in range(PEERS):
        out[d] = tall[SLAB * d : SLAB * d + PAD, :].astype(bf16)


def from_slabs(slabs, tall):
    for d in range(PEERS):
        tall[SLAB * d : SLAB * d + PAD, :] = slabs[d].astype(f32)


def mlp_kernel(tok, cot, w_in, w_out, send, hidden, pre_grad, acc, tall):
    step = pl.program_id(0)
    last = pl.num_programs(0) - 1
    gelu_value, slope = gelu_parts(nn(tok[...], w_in[...]))
    hidden[...] = gelu_value.astype(bf16)
    grad = (nt(cot[...], w_out[...]) * slope).astype(bf16)
    pre_grad[...] = grad

    @pl.when(step == 0)
    def _():
        acc[...] = cot[...].astype(f32).T

    acc[...] += nt(w_in[...], grad)

    @pl.when(step == last)
    def _():
        tall[TALL - 8 :, :] = jnp.zeros((8, 128), f32)
        for j in range(GROUPS):
            for a in range(LONS // 4):
                tiles = [acc[(4 * j + q) * 32 : (4 * j + q + 1) * 32, a * 128 : (a + 1) * 128] for q in range(4)]
                for b, tile in enumerate(swap_quarters(tiles)):
                    tall[pl.ds((4 * a + b) * GROUPS + j, PEERS, stride=SLAB), :] = tile
        to_slabs(tall, send)


def grads_kernel(core, tok, cot, hidden, pre_grad, mine, theirs, tok_t, cot_t, scr):
    @pl.when(pl.program_id(0) == 0)
    def _():
        tok_t[...] = tok[...].astype(f32).T.astype(bf16)
        cot_t[...] = cot[...].astype(f32).T.astype(bf16)

    c = core[0]
    depth, _, size = mine.shape[0], mine.shape[1], mine.shape[2]
    for which, (left, right) in enumerate(((tok_t, pre_grad), (cot_t, hidden))):
        scr[...] = nn(left[...], right[...])
        for z in range(depth):
            own = pl.multiple_of((2 * z + c) * size, 8)
            other = pl.multiple_of((2 * z + 1 - c) * size, 8)
            mine[z, which] = scr[pl.ds(own, size), :].astype(bf16)
            theirs[z, which] = scr[pl.ds(other, size), :].astype(bf16)


def prep_kernel(place, row_w, cols, widths, chan, basis, own_mix, rim_mix, spread, coefs):
    row_start, lon = place[0], place[1]
    high = lax.Precision.HIGHEST
    count = cols.shape[1]
    at = lax.broadcasted_iota(jnp.int32, (64, count), 0)
    rim = at % 4
    source = jnp.where(at < 32, at, jnp.where(at < 48, rim - REACH, rim + ROWS)) + row_start
    pick = (source == lax.broadcasted_iota(jnp.int32, (64, count), 1)).astype(f32)
    col = nt(pick, cols[...].astype(f32), high) - row_start.astype(f32)
    width = nt(pick, widths[...].astype(f32), high)
    lane = lax.broadcasted_iota(jnp.int32, (64, 128), 1)
    target = (lane % 32).astype(f32)
    hits = [
        jnp.where((col[:, s : s + 1] == target) & (width > s), 1.0, 0.0) for s in range(NB)
    ]
    chan_row = lax.broadcasted_iota(jnp.int32, (640, 640), 0)
    chan_lane = lax.broadcasted_iota(jnp.int32, (640, 640), 1)
    chan_pick = (chan_row == (chan_lane // 32) * 32 + lon).astype(f32)
    chan_w = nn(chan[...], chan_pick, high)
    rim_mix[...] = jnp.zeros(rim_mix.shape, bf16)
    quarter = lane[:32] // 32
    rim_at = lax.broadcasted_iota(jnp.int32, (16, 128), 0) // 4
    rim_quarter = lane[:16] // 32
    for k in range(NB):
        coef = nt(pick, row_w[k], high)
        weight = None
        for s in range(NB):
            term = coef[:, s : s + 1] * hits[s]
            weight = term if weight is None else weight + term
        for j in range(GROUPS):
            scaled = weight * chan_w[k : k + 1, 128 * j : 128 * (j + 1)]
            for q in range(4):
                own_mix[j, k * 128 + q * 32 : k * 128 + (q + 1) * 32, :] = jnp.where(
                    quarter == q, scaled[:32], 0.0
                ).astype(bf16)
            for side in range(2):
                part = scaled[32 + 16 * side : 48 + 16 * side]
                start = (k * 2 + side) * 128 + 16 * j
                rim_mix[start : start + 16, 128 * j : 128 * (j + 1)] = jnp.where(
                    rim_quarter == rim_at, part, 0.0
                ).astype(bf16)
        spread[k] = jnp.broadcast_to(basis[k : k + 1, :], (128, NLON)).T


def open_kernel(slabs, pick, moved, rims, tall):
    from_slabs(slabs, tall)
    for j in range(GROUPS):
        moved[:, 128 * j : 128 * (j + 1)] = tall[pl.ds(j, NLON, stride=GROUPS), :].astype(bf16)
    edges = nn(moved[...], pick[...]).astype(bf16)
    rims[0] = edges[:, :128]
    rims[1] = edges[:, 128:]


def own_kernel(moved, forward, spread, own_mix, filtered, mixed):
    spectra = nn(forward[...], moved[...])
    first, second = spectra[:NF], spectra[NF:]
    for k in range(NB):
        cosine, sine = spread[k, :NF], spread[k, NF:]
        mixed[:NF, k * 128 : (k + 1) * 128] = (cosine * first + sine * second).astype(bf16)
        mixed[NF:, k * 128 : (k + 1) * 128] = (cosine * second - sine * first).astype(bf16)
    filtered[...] = nn(mixed[...], own_mix[0])


def close_kernel(filtered, before, after, forward, inverse, spread, rim_mix, send, mixed, tall):
    for side, rim in enumerate((before, after)):
        spectra = nn(forward[...], rim[...])
        first, second = spectra[:NF], spectra[NF:]
        for k in range(NB):
            cosine, sine = spread[k, :NF], spread[k, NF:]
            at = (k * 2 + side) * 128
            mixed[:NF, at : at + 128] = (cosine * first + sine * second).astype(bf16)
            mixed[NF:, at : at + 128] = (cosine * second - sine * first).astype(bf16)
    whole = (filtered[...] + nn(mixed[...], rim_mix[...])).astype(bf16)
    tall[TALL - 8 :, :] = jnp.zeros((8, 128), f32)
    for j in range(GROUPS):
        tall[pl.ds(j, NLON, stride=GROUPS), :] = nn(inverse[...], whole[:, 128 * j : 128 * (j + 1)])
    to_slabs(tall, send)


def final_kernel(slabs, cot, out, tall):
    from_slabs(slabs, tall)
    for j in range(GROUPS):
        for a in range(LONS // 4):
            tiles = [tall[pl.ds((4 * a + b) * GROUPS + j, PEERS, stride=SLAB), :] for b in range(4)]
            turned = jnp.concatenate(tiles, 0).T
            for b, tile in enumerate(swap_quarters([turned[32 * q : 32 * (q + 1)] for q in range(4)])):
                rows = slice((4 * a + b) * 32, (4 * a + b + 1) * 32)
                lanes = slice(128 * j, 128 * (j + 1))
                out[rows, lanes] = (cot[rows, lanes].astype(f32) + tile).astype(bf16)


def turn_kernel(block, out):
    rows = block[0].astype(f32), block[1].astype(f32)
    size = rows[0].shape[0]
    fill = jnp.zeros((-(2 * size) % 128, rows[0].shape[1]), f32)
    out[...] = jnp.concatenate([rows[0], rows[1], fill], 0).T.astype(bf16)


def sum_kernel(parts, grad_in, grad_out):
    total = parts[0].astype(f32)
    for d in range(1, parts.shape[0]):
        total = total + parts[d].astype(f32)
    size = grad_in.shape[0]
    lanes = total.shape[1]
    filled = jnp.concatenate([total, jnp.zeros((-total.shape[0] % 128, lanes), f32)], 0)
    grad_in[...] = filled.T[:size, : grad_in.shape[1]]
    grad_out[...] = total[:, size : 2 * size]


def tables():
    lon = np.arange(NLON)
    freq = np.arange(NLON) % NF
    phase = (lon[:, None] * freq[None, :] % NLON) * (2.0 * math.pi / NLON)
    forward = np.where(np.arange(NLON)[None, :] >= NF, np.sin(phase), np.cos(phase))
    inverse = forward.T * (np.where(freq == 0, 1.0, 2.0) / NLON)[:, None]
    return jnp.asarray(forward.T, bf16), jnp.asarray(inverse.T, bf16)


def rim_picks():
    pick = np.zeros((640, 256), np.float32)
    for c in range(LOCAL):
        for r in range(REACH):
            pick[c * 32 + ROWS - REACH + r, c * 4 + r] = 1.0
            pick[c * 32 + r, 128 + c * 4 + r] = 1.0
    return jnp.asarray(pick, bf16)


def shape(*dims, dtype=bf16):
    return jax.ShapeDtypeStruct(dims, dtype)


VMEM = pl.BlockSpec(memory_space=pltpu.VMEM)
SMEM = pl.BlockSpec(memory_space=pltpu.SMEM)


def call(kernel, out, ins, flops, moved, scratch=(), **grid):
    options = dict(grid)
    if "grid" not in options:
        options["in_specs"] = ins
        options["out_specs"] = jax.tree.map(lambda _: VMEM, out)
    return pl.pallas_call(
        kernel,
        out_shape=out,
        scratch_shapes=list(scratch),
        compiler_params=pltpu.CompilerParams(vmem_limit_bytes=40 << 20),
        cost_estimate=pl.CostEstimate(flops=int(flops), bytes_accessed=int(moved), transcendentals=0),
        **options,
    )


def body(mlp_input, out_cot, w_in, w_out, chan_weights, row_weights, basis_spectra, band_cols, band_widths):
    tokens_n = ROWS * LONS
    depth = lax.axis_size("z")
    n_lat = depth * lax.axis_size("core")
    part = 640 // n_lat
    lat, lon, core = lax.axis_index(LAT), lax.axis_index(LON), lax.axis_index("core")
    tokens = mlp_input.transpose(1, 0, 2).reshape(tokens_n, 640)
    cotangent = out_cot.transpose(1, 0, 2).reshape(tokens_n, 640)
    whole = lambda *dims: pl.BlockSpec(dims, lambda i: (0,) * len(dims))

    send, hidden, pre_grad = call(
        mlp_kernel,
        (shape(PEERS, PAD, 128), shape(tokens_n, 1280), shape(tokens_n, 1280)),
        None,
        2e9,
        6e6,
        [pltpu.VMEM((640, tokens_n), f32), pltpu.VMEM((TALL, 128), f32)],
        grid=(5,),
        in_specs=[
            whole(tokens_n, 640),
            whole(tokens_n, 640),
            pl.BlockSpec((640, 256), lambda i: (0, i)),
            pl.BlockSpec((256, 640), lambda i: (i, 0)),
        ],
        out_specs=[
            whole(PEERS, PAD, 128),
            pl.BlockSpec((tokens_n, 256), lambda i: (0, i)),
            pl.BlockSpec((tokens_n, 256), lambda i: (0, i)),
        ],
    )(tokens, cotangent, w_in, w_out)

    received = lax.all_to_all(send, LON, split_axis=0, concat_axis=0, tiled=True)

    half = shape(depth, 2, part, 1280)
    half_spec = pl.BlockSpec((depth, 2, part, 256), lambda i: (0, 0, 0, i))
    wide = pl.BlockSpec((tokens_n, 256), lambda i: (0, i))
    mine, theirs = call(
        grads_kernel,
        (half, half),
        None,
        1.3e9,
        8e6,
        [pltpu.VMEM((640, tokens_n), bf16), pltpu.VMEM((640, tokens_n), bf16), pltpu.VMEM((640, 256), f32)],
        grid=(5,),
        in_specs=[SMEM, whole(tokens_n, 640), whole(tokens_n, 640), wide, wide],
        out_specs=[half_spec, half_spec],
    )(core.reshape(1), tokens, cotangent, hidden, pre_grad)
    partner = lax.ppermute(theirs, "core", [(0, 1), (1, 0)])
    chip = (mine.astype(f32) + partner.astype(f32)).astype(bf16)
    column = lax.psum_scatter(chip, "z", scatter_dimension=0, tiled=True)

    own_mix, rim_mix, spread = call(
        prep_kernel,
        (shape(GROUPS, NB * 128, 128), shape(NB * 256, 640), shape(NB, NLON, 128, dtype=f32)),
        [SMEM] + [VMEM] * 5,
        1e9,
        6e6,
        [pltpu.VMEM((8, 128), f32)],
    )(
        jnp.stack([lat * ROWS, lon]).astype(jnp.int32),
        row_weights.transpose(0, 2, 1),
        band_cols.T,
        band_widths.reshape(1, -1),
        chan_weights,
        basis_spectra,
    )

    forward, inverse = tables()
    moved, rims = call(
        open_kernel,
        (shape(NLON, 640), shape(2, NLON, 128)),
        [VMEM] * 2,
        1e8,
        2e6,
        [pltpu.VMEM((TALL, 128), f32)],
    )(received, rim_picks())
    up = [(i, i + 1) for i in range(n_lat - 1)]
    before = lax.ppermute(rims[0], LAT, up)
    after = lax.ppermute(rims[1], LAT, [(b, a) for a, b in up])

    filtered = call(
        own_kernel,
        shape(NLON, 640, dtype=f32),
        None,
        8e8,
        5e6,
        [pltpu.VMEM((NLON, NB * 128), bf16)],
        grid=(GROUPS,),
        in_specs=[
            pl.BlockSpec((NLON, 128), lambda j: (0, j)),
            whole(NLON, NLON),
            whole(NB, NLON, 128),
            pl.BlockSpec((1, NB * 128, 128), lambda j: (j, 0, 0)),
        ],
        out_specs=pl.BlockSpec((NLON, 128), lambda j: (0, j)),
    )(moved, forward, spread, own_mix)

    answer = call(
        close_kernel,
        shape(PEERS, PAD, 128),
        [VMEM] * 7,
        1.5e9,
        7e6,
        [pltpu.VMEM((NLON, NB * 256), bf16), pltpu.VMEM((TALL, 128), f32)],
    )(filtered, before, after, forward, inverse, spread, rim_mix)
    returned = lax.all_to_all(answer, LON, split_axis=0, concat_axis=0, tiled=True)
    grid_grad = call(
        final_kernel, shape(tokens_n, 640), [VMEM] * 2, 1e8, 2e6, [pltpu.VMEM((TALL, 128), f32)]
    )(returned, cotangent)
    grid_grad = grid_grad.reshape(LONS, ROWS, 640).transpose(1, 0, 2)

    lanes = -(-2 * part // 128) * 128
    turned = call(turn_kernel, shape(1280, lanes), [VMEM], 1e6, 1e6)(column.reshape(2, part, 1280))
    pieces = lax.all_to_all(
        turned.reshape(PEERS, 1280 // PEERS, lanes), LON, split_axis=0, concat_axis=0, tiled=True
    )
    grad_in, grad_out = call(
        sum_kernel,
        (shape(part, 1280 // PEERS, dtype=f32), shape(1280 // PEERS, part, dtype=f32)),
        [VMEM],
        1e6,
        1e6,
    )(pieces)
    return grid_grad, grad_in, grad_out


def solution(mesh):
    chips = Mesh(mesh.devices.reshape(-1, 2, 8, 4), ("z", "core", "y", "x"))
    grid = P(LAT, LON, None)
    return jax.shard_map(
        body,
        mesh=chips,
        in_specs=(grid, grid, P(), P(), P(), P(), P(), P(), P()),
        out_specs=(grid, P(LAT, LON), P(LON, LAT)),
        check_vma=False,
    )
```

```python
import functools
import math

import jax
import jax.numpy as jnp
import numpy as np
from jax import lax
from jax.experimental import pallas as pl
from jax.experimental.pallas import tpu as pltpu
from jax.sharding import Mesh, PartitionSpec as P

f32 = jnp.float32
bf16 = jnp.bfloat16
LAT = ("z", "core")
LON = ("y", "x")
ROWS = 32
LONS = 12
PEERS = 32
LOCAL = 20
NLON = 384
NF = 192
NB = 9
REACH = 4
GROUPS = 5
SLAB = LONS * GROUPS
PAD = 64
TALL = PEERS * SLAB + 8


def nt(a, b, precision=None):
    return lax.dot_general(a, b, (((1,), (1,)), ((), ())), preferred_element_type=f32, precision=precision)


def tn(a, b):
    return lax.dot_general(a, b, (((0,), (0,)), ((), ())), preferred_element_type=f32)


def nn(a, b, precision=None):
    return lax.dot_general(a, b, (((1,), (0,)), ((), ())), preferred_element_type=f32, precision=precision)


def swap_quarters(tiles):
    quarter = lax.broadcasted_iota(jnp.int32, tiles[0].shape, 1) // 32
    out = []
    for b in range(4):
        made = None
        for q in range(4):
            shift = (32 * (q - b)) % 128
            moved = pltpu.roll(tiles[q], shift, 1) if shift else tiles[q]
            made = moved if made is None else jnp.where(quarter == q, moved, made)
        out.append(made)
    return out


def gelu_parts(v):
    square = v * v
    tangent = jnp.tanh(0.7978845608 * (v + 0.044715 * v * square))
    half = 0.5 * (1.0 + tangent)
    slope = half + 0.5 * v * (1.0 - tangent * tangent) * 0.7978845608 * (1.0 + 0.134145 * square)
    return v * half, slope


def to_slabs(tall, out):
    for d in range(PEERS):
        out[d] = tall[SLAB * d : SLAB * d + PAD, :].astype(bf16)


def from_slabs(slabs, tall):
    for d in range(PEERS):
        tall[SLAB * d : SLAB * d + PAD, :] = slabs[d].astype(f32)


def head_kernel(core, tok, cot, w_in, w_out, pre_grad, mine, theirs, tok_t, cot_t, scr):
    @pl.when(pl.program_id(0) == 0)
    def _():
        tok_t[...] = tok[...].astype(f32).T.astype(bf16)
        cot_t[...] = cot[...].astype(f32).T.astype(bf16)

    gelu_value, slope = gelu_parts(nn(tok[...], w_in[...]))
    grad = (nt(cot[...], w_out[...]) * slope).astype(bf16)
    pre_grad[...] = grad
    c = core[0]
    depth, _, size = mine.shape[0], mine.shape[1], mine.shape[2]
    for which, (left, right) in enumerate(((tok_t, grad), (cot_t, gelu_value.astype(bf16)))):
        scr[which] = nn(left[...], right)
        for z in range(depth):
            own = pl.multiple_of((2 * z + c) * size, 8)
            other = pl.multiple_of((2 * z + 1 - c) * size, 8)
            mine[z, which] = scr[which, pl.ds(own, size), :].astype(bf16)
            theirs[z, which] = scr[which, pl.ds(other, size), :].astype(bf16)


def lift_kernel(pre_grad, cot, w_in, send, tall):
    j = pl.program_id(0)
    whole = cot[...].astype(f32).T + nt(w_in[...], pre_grad[...])
    for a in range(LONS // 4):
        tiles = [whole[q * 32 : (q + 1) * 32, a * 128 : (a + 1) * 128] for q in range(4)]
        for b, tile in enumerate(swap_quarters(tiles)):
            tall[pl.ds((4 * a + b) * GROUPS + j, PEERS, stride=SLAB), :] = tile

    @pl.when(j == pl.num_programs(0) - 1)
    def _():
        tall[TALL - 8 :, :] = jnp.zeros((8, 128), f32)
        to_slabs(tall, send)


def add_kernel(one, two, out):
    for z in range(one.shape[0]):
        for w in range(one.shape[1]):
            out[z, w] = (one[z, w].astype(f32) + two[z, w].astype(f32)).astype(bf16)


def prep_kernel(place, row_w, cols, widths, chan, own_mix, rim_mix, token):
    token[...] = jnp.zeros(token.shape, f32)
    row_start, lon = place[0], place[1]
    high = lax.Precision.HIGHEST
    count = cols.shape[1]
    at = lax.broadcasted_iota(jnp.int32, (64, count), 0)
    rim = at % 4
    source = jnp.where(at < 32, at, jnp.where(at < 48, rim - REACH, rim + ROWS)) + row_start
    pick = (source == lax.broadcasted_iota(jnp.int32, (64, count), 1)).astype(f32)
    col = nt(pick, cols[...].astype(f32), high) - row_start.astype(f32)
    width = nt(pick, widths[...].astype(f32), high)
    lane = lax.broadcasted_iota(jnp.int32, (64, 128), 1)
    target = (lane % 32).astype(f32)
    hits = [
        jnp.where((col[:, s : s + 1] == target) & (width > s), 1.0, 0.0) for s in range(NB)
    ]
    chan_row = lax.broadcasted_iota(jnp.int32, (640, 640), 0)
    chan_lane = lax.broadcasted_iota(jnp.int32, (640, 640), 1)
    chan_pick = (chan_row == (chan_lane // 32) * 32 + lon).astype(f32)
    chan_w = nn(chan[...], chan_pick, high)
    rim_mix[...] = jnp.zeros(rim_mix.shape, bf16)
    quarter = lane[:32] // 32
    rim_at = lax.broadcasted_iota(jnp.int32, (16, 128), 0) // 4
    rim_quarter = lane[:16] // 32
    for k in range(NB):
        coef = nt(pick, row_w[k], high)
        weight = None
        for s in range(NB):
            term = coef[:, s : s + 1] * hits[s]
            weight = term if weight is None else weight + term
        for j in range(GROUPS):
            scaled = weight * chan_w[k : k + 1, 128 * j : 128 * (j + 1)]
            for q in range(4):
                own_mix[j, k * 128 + q * 32 : k * 128 + (q + 1) * 32, :] = jnp.where(
                    quarter == q, scaled[:32], 0.0
                ).astype(bf16)
            for side in range(2):
                part = scaled[32 + 16 * side : 48 + 16 * side]
                start = (k * 2 + side) * 128 + 16 * j
                rim_mix[start : start + 16, 128 * j : 128 * (j + 1)] = jnp.where(
                    rim_quarter == rim_at, part, 0.0
                ).astype(bf16)


def open_kernel(slabs, pick, _ready, moved, first, last, tall):
    from_slabs(slabs, tall)
    for j in range(GROUPS):
        moved[:, 128 * j : 128 * (j + 1)] = tall[pl.ds(j, NLON, stride=GROUPS), :].astype(bf16)
    edges = nn(moved[...], pick[...]).astype(bf16)
    last[...] = edges[:, :128]
    first[...] = edges[:, 128:]


def mix(spectra, basis_t, mixed, step, start):
    first, second = spectra[:NF], spectra[NF:]
    lanes = spectra.shape[1]
    for k in range(NB):
        cosine = jnp.broadcast_to(basis_t[:NF, k : k + 1], (NF, lanes))
        sine = jnp.broadcast_to(basis_t[NF:, k : k + 1], (NF, lanes))
        at = start + step * k
        mixed[:NF, at : at + lanes] = (cosine * first + sine * second).astype(bf16)
        mixed[NF:, at : at + lanes] = (cosine * second - sine * first).astype(bf16)


def turned_basis(basis):
    return jnp.concatenate([basis[...], jnp.zeros((128 - NB, NLON), f32)], 0).T


def own_kernel(moved, forward, basis, own_mix, filtered, mixed, held, sems):
    copies = [pltpu.make_async_copy(own_mix.at[j], held.at[j], sems.at[j]) for j in range(GROUPS)]
    for copy in copies:
        copy.start()
    basis_t = turned_basis(basis)
    for j in range(GROUPS):
        lanes = slice(128 * j, 128 * (j + 1))
        mix(nn(forward[...], moved[:, lanes]), basis_t, mixed.at[j % 2], 128, 0)
        copies[j].wait()
        filtered[:, lanes] = nn(mixed[j % 2], held[j])


def close_kernel(filtered, before, after, forward, inverse, basis, rim_mix, send, mixed, tall, held, sem):
    copy = pltpu.make_async_copy(rim_mix, held, sem)
    copy.start()
    basis_t = turned_basis(basis)
    for side, rim in enumerate((before, after)):
        mix(nn(forward[...], rim[...]), basis_t, mixed, 256, 128 * side)
    tall[TALL - 8 :, :] = jnp.zeros((8, 128), f32)
    copy.wait()
    for j in range(GROUPS):
        lanes = slice(128 * j, 128 * (j + 1))
        whole = (filtered[:, lanes] + nn(mixed[...], held[:, lanes])).astype(bf16)
        tall[pl.ds(j, NLON, stride=GROUPS), :] = nn(inverse[...], whole)
    to_slabs(tall, send)


def merge_kernel(answer, column, out):
    rows = column[0, 0].astype(f32), column[0, 1].astype(f32)
    fill = jnp.zeros((-(2 * rows[0].shape[0]) % 128, rows[0].shape[1]), f32)
    turned = jnp.concatenate([rows[0], rows[1], fill], 0).T
    for d in range(PEERS):
        out[d, :PAD] = answer[d]
        for i in range(turned.shape[1] // 128):
            out[d, PAD + 40 * i : PAD + 40 * (i + 1)] = turned[40 * d : 40 * (d + 1), 128 * i : 128 * (i + 1)].astype(bf16)


def final_kernel(slabs, cot, out, grad_in, grad_out, tall):
    for d in range(PEERS):
        tall[SLAB * d : SLAB * d + PAD, :] = slabs[d, :PAD].astype(f32)
    for j in range(GROUPS):
        for a in range(LONS // 4):
            tiles = [tall[pl.ds((4 * a + b) * GROUPS + j, PEERS, stride=SLAB), :] for b in range(4)]
            turned = jnp.concatenate(tiles, 0).T
            for b, tile in enumerate(swap_quarters([turned[32 * q : 32 * (q + 1)] for q in range(4)])):
                rows = slice((4 * a + b) * 32, (4 * a + b + 1) * 32)
                lanes = slice(128 * j, 128 * (j + 1))
                out[rows, lanes] = (cot[rows, lanes].astype(f32) + tile).astype(bf16)
    size = grad_in.shape[0]
    total = slabs[0, PAD:].astype(f32)
    for d in range(1, PEERS):
        total = total + slabs[d, PAD:].astype(f32)
    if total.shape[0] > 40:
        total = jnp.concatenate([total[i : i + 40] for i in range(0, total.shape[0], 40)], 1)
    lanes = total.shape[1]
    filled = jnp.concatenate([total, jnp.zeros((128 - 40, lanes), f32)], 0)
    grad_in[...] = filled.T[:size, :40]
    grad_out[...] = total[:, size : 2 * size]


def tables():
    lon = np.arange(NLON)
    freq = np.arange(NLON) % NF
    phase = (lon[:, None] * freq[None, :] % NLON) * (2.0 * math.pi / NLON)
    forward = np.where(np.arange(NLON)[None, :] >= NF, np.sin(phase), np.cos(phase))
    inverse = forward.T * (np.where(freq == 0, 1.0, 2.0) / NLON)[:, None]
    return jnp.asarray(forward.T, bf16), jnp.asarray(inverse.T, bf16)


def rim_picks():
    pick = np.zeros((640, 256), np.float32)
    for c in range(LOCAL):
        for r in range(REACH):
            pick[c * 32 + ROWS - REACH + r, c * 4 + r] = 1.0
            pick[c * 32 + r, 128 + c * 4 + r] = 1.0
    return jnp.asarray(pick, bf16)


def shape(*dims, dtype=bf16):
    return jax.ShapeDtypeStruct(dims, dtype)


VMEM = pl.BlockSpec(memory_space=pltpu.VMEM)
TOKEN = shape(8, 128, dtype=f32)
HBM = pl.BlockSpec(memory_space=pltpu.HBM)
SMEM = pl.BlockSpec(memory_space=pltpu.SMEM)


def call(kernel, out, ins, flops, moved, scratch=(), limit=24, **grid):
    options = dict(grid)
    if "grid" not in options:
        options["in_specs"] = ins
        options["out_specs"] = jax.tree.map(lambda _: VMEM, out)
    return pl.pallas_call(
        kernel,
        out_shape=out,
        scratch_shapes=list(scratch),
        compiler_params=pltpu.CompilerParams(vmem_limit_bytes=limit << 20),
        cost_estimate=pl.CostEstimate(flops=int(flops), bytes_accessed=int(moved), transcendentals=0),
        **options,
    )


def body(mlp_input, out_cot, w_in, w_out, chan_weights, row_weights, basis_spectra, band_cols, band_widths):
    tokens_n = ROWS * LONS
    depth = lax.axis_size("z")
    n_lat = depth * lax.axis_size("core")
    part = 640 // n_lat
    lat, lon, core = lax.axis_index(LAT), lax.axis_index(LON), lax.axis_index("core")
    tokens = mlp_input.transpose(1, 0, 2).reshape(tokens_n, 640)
    cotangent = out_cot.transpose(1, 0, 2).reshape(tokens_n, 640)
    whole = lambda *dims: pl.BlockSpec(dims, lambda i: (0,) * len(dims))

    half = shape(depth, 2, part, 1280)
    half_spec = pl.BlockSpec((depth, 2, part, 256), lambda i: (0, 0, 0, i))
    pre_grad, mine, theirs = call(
        head_kernel,
        (shape(tokens_n, 1280), half, half),
        None,
        3e9,
        8e6,
        [pltpu.VMEM((640, tokens_n), bf16), pltpu.VMEM((640, tokens_n), bf16), pltpu.VMEM((2, 640, 256), f32)],
        limit=62,
        grid=(5,),
        in_specs=[
            SMEM,
            whole(tokens_n, 640),
            whole(tokens_n, 640),
            pl.BlockSpec((640, 256), lambda i: (0, i)),
            pl.BlockSpec((256, 640), lambda i: (i, 0)),
        ],
        out_specs=[pl.BlockSpec((tokens_n, 256), lambda i: (0, i)), half_spec, half_spec],
    )(core.reshape(1), tokens, cotangent, w_in, w_out)
    partner = lax.ppermute(theirs, "core", [(0, 1), (1, 0)])

    send = call(
        lift_kernel,
        shape(PEERS, PAD, 128),
        None,
        2e9,
        4e6,
        [pltpu.VMEM((TALL, 128), f32)],
        limit=62,
        grid=(GROUPS,),
        in_specs=[
            whole(tokens_n, 1280),
            pl.BlockSpec((tokens_n, 128), lambda j: (0, j)),
            pl.BlockSpec((128, 1280), lambda j: (j, 0)),
        ],
        out_specs=whole(PEERS, PAD, 128),
    )(pre_grad, cotangent, w_in)
    received = lax.all_to_all(send, LON, split_axis=0, concat_axis=0, tiled=True)

    slab = pl.BlockSpec((1, 2, part, 1280), lambda i: (i, 0, 0, 0))
    chip = call(
        add_kernel, half, None, 1e6, 5e6, limit=62, grid=(depth,), in_specs=[slab] * 2, out_specs=slab
    )(mine, partner)
    column = lax.psum_scatter(chip, "z", scatter_dimension=0, tiled=True)

    own_mix, rim_mix, ready = call(
        prep_kernel,
        (shape(GROUPS, NB * 128, 128), shape(NB * 256, 640), TOKEN),
        [SMEM] + [VMEM] * 4,
        1e9,
        6e6,
        limit=62,
    )(
        jnp.stack([lat * ROWS, lon]).astype(jnp.int32),
        row_weights.transpose(0, 2, 1),
        band_cols.T,
        band_widths.reshape(1, -1),
        chan_weights,
    )

    forward, inverse = tables()
    moved, first, last = call(
        open_kernel,
        (shape(NLON, 640), shape(NLON, 128), shape(NLON, 128)),
        [VMEM] * 3,
        1e8,
        2e6,
        [pltpu.VMEM((TALL, 128), f32)],
    )(received, rim_picks(), ready)
    up = [(i, i + 1) for i in range(n_lat - 1)]
    before = lax.ppermute(last, LAT, up)
    after = lax.ppermute(first, LAT, [(b, a) for a, b in up])

    filtered = call(
        own_kernel,
        shape(NLON, 640, dtype=f32),
        [VMEM] * 3 + [HBM],
        8e8,
        5e6,
        [
            pltpu.VMEM((2, NLON, NB * 128), bf16),
            pltpu.VMEM((GROUPS, NB * 128, 128), bf16),
            pltpu.SemaphoreType.DMA((GROUPS,)),
        ],
        limit=62,
    )(moved, forward, basis_spectra, own_mix)

    answer = call(
        close_kernel,
        shape(PEERS, PAD, 128),
        [VMEM] * 6 + [HBM],
        1.5e9,
        7e6,
        [
            pltpu.VMEM((NLON, NB * 256), bf16),
            pltpu.VMEM((TALL, 128), f32),
            pltpu.VMEM((NB * 256, 640), bf16),
            pltpu.SemaphoreType.DMA,
        ],
        limit=62,
    )(filtered, before, after, forward, inverse, basis_spectra, rim_mix)
    tall = PAD + 40 * -(-2 * part // 128)
    merged = call(merge_kernel, shape(PEERS, tall, 128), [VMEM] * 2, 1e6, 2e6, limit=62)(answer, column)
    returned = lax.all_to_all(merged, LON, split_axis=0, concat_axis=0, tiled=True)
    grid_grad, grad_in, grad_out = call(
        final_kernel,
        (shape(tokens_n, 640), shape(part, 40, dtype=f32), shape(40, part, dtype=f32)),
        [VMEM] * 2,
        1e8,
        2e6,
        [pltpu.VMEM((TALL, 128), f32)],
    )(returned, cotangent)
    grid_grad = grid_grad.reshape(LONS, ROWS, 640).transpose(1, 0, 2)
    return grid_grad, grad_in, grad_out


def solution(mesh):
    chips = Mesh(mesh.devices.reshape(-1, 2, 8, 4), ("z", "core", "y", "x"))
    grid = P(LAT, LON, None)
    return jax.shard_map(
        body,
        mesh=chips,
        in_specs=(grid, grid, P(), P(), P(), P(), P(), P(), P()),
        out_specs=(grid, P(LAT, LON), P(LON, LAT)),
        check_vma=False,
    )
```

```python
import functools
import math

import jax
import jax.numpy as jnp
import numpy as np
from jax import lax
from jax.experimental import pallas as pl
from jax.experimental.pallas import tpu as pltpu
from jax.sharding import Mesh, PartitionSpec as P

f32 = jnp.float32
bf16 = jnp.bfloat16
LAT = ("z", "core")
LON = ("y", "x")
ROWS = 32
LONS = 12
PEERS = 32
LOCAL = 20
NLON = 384
NF = 192
NB = 9
REACH = 4
GROUPS = 5
SLAB = LONS * GROUPS
PAD = 64
TALL = PEERS * SLAB + 8


def nt(a, b, precision=None):
    return lax.dot_general(a, b, (((1,), (1,)), ((), ())), preferred_element_type=f32, precision=precision)


def tn(a, b):
    return lax.dot_general(a, b, (((0,), (0,)), ((), ())), preferred_element_type=f32)


def nn(a, b, precision=None):
    return lax.dot_general(a, b, (((1,), (0,)), ((), ())), preferred_element_type=f32, precision=precision)


def swap_quarters(tiles):
    quarter = lax.broadcasted_iota(jnp.int32, tiles[0].shape, 1) // 32
    out = []
    for b in range(4):
        made = None
        for q in range(4):
            shift = (32 * (q - b)) % 128
            moved = pltpu.roll(tiles[q], shift, 1) if shift else tiles[q]
            made = moved if made is None else jnp.where(quarter == q, moved, made)
        out.append(made)
    return out


def gelu_parts(v):
    square = v * v
    tangent = jnp.tanh(0.7978845608 * (v + 0.044715 * v * square))
    half = 0.5 * (1.0 + tangent)
    slope = half + 0.5 * v * (1.0 - tangent * tangent) * 0.7978845608 * (1.0 + 0.134145 * square)
    return v * half, slope


def to_slabs(tall, out):
    for d in range(PEERS):
        out[d] = tall[SLAB * d : SLAB * d + PAD, :].astype(bf16)


def from_slabs(slabs, tall):
    for d in range(PEERS):
        tall[SLAB * d : SLAB * d + PAD, :] = slabs[d].astype(f32)


def head_kernel(core, tok, cot, w_in, w_out, pre_grad, mine, theirs, tok_t, cot_t, scr):
    @pl.when(pl.program_id(0) == 0)
    def _():
        tok_t[...] = tok[...].astype(f32).T.astype(bf16)
        cot_t[...] = cot[...].astype(f32).T.astype(bf16)

    gelu_value, slope = gelu_parts(nn(tok[...], w_in[...]))
    grad = (nt(cot[...], w_out[...]) * slope).astype(bf16)
    pre_grad[...] = grad
    c = core[0]
    depth, _, size = mine.shape[0], mine.shape[1], mine.shape[2]
    for which, (left, right) in enumerate(((tok_t, grad), (cot_t, gelu_value.astype(bf16)))):
        scr[which] = nn(left[...], right)
        for z in range(depth):
            own = pl.multiple_of((2 * z + c) * size, 8)
            other = pl.multiple_of((2 * z + 1 - c) * size, 8)
            mine[z, which] = scr[which, pl.ds(own, size), :].astype(bf16)
            theirs[z, which] = scr[which, pl.ds(other, size), :].astype(bf16)


def lift_kernel(pre_grad, cot, w_in, send, tall):
    j = pl.program_id(0)
    whole = cot[...].astype(f32).T + nt(w_in[...], pre_grad[...])
    for a in range(LONS // 4):
        tiles = [whole[q * 32 : (q + 1) * 32, a * 128 : (a + 1) * 128] for q in range(4)]
        for b, tile in enumerate(swap_quarters(tiles)):
            tall[pl.ds((4 * a + b) * GROUPS + j, PEERS, stride=SLAB), :] = tile

    @pl.when(j == pl.num_programs(0) - 1)
    def _():
        tall[TALL - 8 :, :] = jnp.zeros((8, 128), f32)
        to_slabs(tall, send)


def prep_kernel(place, row_w, cols, widths, chan, basis, own_mix, rim_mix, spread, token):
    token[...] = jnp.zeros(token.shape, f32)
    row_start, lon = place[0], place[1]
    high = lax.Precision.HIGHEST
    count = cols.shape[1]
    at = lax.broadcasted_iota(jnp.int32, (64, count), 0)
    rim = at % 4
    source = jnp.where(at < 32, at, jnp.where(at < 48, rim - REACH, rim + ROWS)) + row_start
    pick = (source == lax.broadcasted_iota(jnp.int32, (64, count), 1)).astype(f32)
    col = nt(pick, cols[...].astype(f32), high) - row_start.astype(f32)
    width = nt(pick, widths[...].astype(f32), high)
    lane = lax.broadcasted_iota(jnp.int32, (64, 128), 1)
    target = (lane % 32).astype(f32)
    hits = [
        jnp.where((col[:, s : s + 1] == target) & (width > s), 1.0, 0.0) for s in range(NB)
    ]
    chan_row = lax.broadcasted_iota(jnp.int32, (640, 640), 0)
    chan_lane = lax.broadcasted_iota(jnp.int32, (640, 640), 1)
    chan_pick = (chan_row == (chan_lane // 32) * 32 + lon).astype(f32)
    chan_w = nn(chan[...], chan_pick, high)
    rim_mix[...] = jnp.zeros(rim_mix.shape, bf16)
    quarter = lane[:32] // 32
    rim_at = lax.broadcasted_iota(jnp.int32, (16, 128), 0) // 4
    rim_quarter = lane[:16] // 32
    for k in range(NB):
        coef = nt(pick, row_w[k], high)
        weight = None
        for s in range(NB):
            term = coef[:, s : s + 1] * hits[s]
            weight = term if weight is None else weight + term
        for j in range(GROUPS):
            scaled = weight * chan_w[k : k + 1, 128 * j : 128 * (j + 1)]
            for q in range(4):
                own_mix[j, k * 128 + q * 32 : k * 128 + (q + 1) * 32, :] = jnp.where(
                    quarter == q, scaled[:32], 0.0
                ).astype(bf16)
            for side in range(2):
                part = scaled[32 + 16 * side : 48 + 16 * side]
                start = (k * 2 + side) * 128 + 16 * j
                rim_mix[start : start + 16, 128 * j : 128 * (j + 1)] = jnp.where(
                    rim_quarter == rim_at, part, 0.0
                ).astype(bf16)
        spread[k] = jnp.broadcast_to(basis[k : k + 1, :], (128, NLON)).T


def open_kernel(slabs, pick, _ready, moved, first, last, tall):
    from_slabs(slabs, tall)
    for j in range(GROUPS):
        moved[:, 128 * j : 128 * (j + 1)] = tall[pl.ds(j, NLON, stride=GROUPS), :].astype(bf16)
    edges = nn(moved[...], pick[...]).astype(bf16)
    last[...] = edges[:, :128]
    first[...] = edges[:, 128:]


def own_kernel(moved, forward, spread, own_mix, filtered, mixed):
    spectra = nn(forward[...], moved[...])
    first, second = spectra[:NF], spectra[NF:]
    for k in range(NB):
        cosine, sine = spread[k, :NF], spread[k, NF:]
        mixed[:NF, k * 128 : (k + 1) * 128] = (cosine * first + sine * second).astype(bf16)
        mixed[NF:, k * 128 : (k + 1) * 128] = (cosine * second - sine * first).astype(bf16)
    filtered[...] = nn(mixed[...], own_mix[0])


def close_kernel(filtered, before, after, forward, inverse, spread, rim_mix, send, mixed, tall):
    for side, rim in enumerate((before, after)):
        spectra = nn(forward[...], rim[...])
        first, second = spectra[:NF], spectra[NF:]
        for k in range(NB):
            cosine, sine = spread[k, :NF], spread[k, NF:]
            at = (k * 2 + side) * 128
            mixed[:NF, at : at + 128] = (cosine * first + sine * second).astype(bf16)
            mixed[NF:, at : at + 128] = (cosine * second - sine * first).astype(bf16)
    whole = (filtered[...] + nn(mixed[...], rim_mix[...])).astype(bf16)
    tall[TALL - 8 :, :] = jnp.zeros((8, 128), f32)
    for j in range(GROUPS):
        tall[pl.ds(j, NLON, stride=GROUPS), :] = nn(inverse[...], whole[:, 128 * j : 128 * (j + 1)])
    to_slabs(tall, send)


def merge_kernel(answer, column, out):
    rows = column[0, 0].astype(f32), column[0, 1].astype(f32)
    fill = jnp.zeros((-(2 * rows[0].shape[0]) % 128, rows[0].shape[1]), f32)
    turned = jnp.concatenate([rows[0], rows[1], fill], 0).T
    for d in range(PEERS):
        out[d, :PAD] = answer[d]
        for i in range(turned.shape[1] // 128):
            out[d, PAD + 40 * i : PAD + 40 * (i + 1)] = turned[40 * d : 40 * (d + 1), 128 * i : 128 * (i + 1)].astype(bf16)


def final_kernel(slabs, cot, out, grad_in, grad_out, tall):
    for d in range(PEERS):
        tall[SLAB * d : SLAB * d + PAD, :] = slabs[d, :PAD].astype(f32)
    for j in range(GROUPS):
        for a in range(LONS // 4):
            tiles = [tall[pl.ds((4 * a + b) * GROUPS + j, PEERS, stride=SLAB), :] for b in range(4)]
            turned = jnp.concatenate(tiles, 0).T
            for b, tile in enumerate(swap_quarters([turned[32 * q : 32 * (q + 1)] for q in range(4)])):
                rows = slice((4 * a + b) * 32, (4 * a + b + 1) * 32)
                lanes = slice(128 * j, 128 * (j + 1))
                out[rows, lanes] = (cot[rows, lanes].astype(f32) + tile).astype(bf16)
    size = grad_in.shape[0]
    total = slabs[0, PAD:].astype(f32)
    for d in range(1, PEERS):
        total = total + slabs[d, PAD:].astype(f32)
    if total.shape[0] > 40:
        total = jnp.concatenate([total[i : i + 40] for i in range(0, total.shape[0], 40)], 1)
    lanes = total.shape[1]
    filled = jnp.concatenate([total, jnp.zeros((128 - 40, lanes), f32)], 0)
    grad_in[...] = filled.T[:size, :40]
    grad_out[...] = total[:, size : 2 * size]


def tables():
    lon = np.arange(NLON)
    freq = np.arange(NLON) % NF
    phase = (lon[:, None] * freq[None, :] % NLON) * (2.0 * math.pi / NLON)
    forward = np.where(np.arange(NLON)[None, :] >= NF, np.sin(phase), np.cos(phase))
    inverse = forward.T * (np.where(freq == 0, 1.0, 2.0) / NLON)[:, None]
    return jnp.asarray(forward.T, bf16), jnp.asarray(inverse.T, bf16)


def rim_picks():
    pick = np.zeros((640, 256), np.float32)
    for c in range(LOCAL):
        for r in range(REACH):
            pick[c * 32 + ROWS - REACH + r, c * 4 + r] = 1.0
            pick[c * 32 + r, 128 + c * 4 + r] = 1.0
    return jnp.asarray(pick, bf16)


def shape(*dims, dtype=bf16):
    return jax.ShapeDtypeStruct(dims, dtype)


VMEM = pl.BlockSpec(memory_space=pltpu.VMEM)
TOKEN = shape(8, 128, dtype=f32)
SMEM = pl.BlockSpec(memory_space=pltpu.SMEM)


def call(kernel, out, ins, flops, moved, scratch=(), limit=24, **grid):
    options = dict(grid)
    if "grid" not in options:
        options["in_specs"] = ins
        options["out_specs"] = jax.tree.map(lambda _: VMEM, out)
    return pl.pallas_call(
        kernel,
        out_shape=out,
        scratch_shapes=list(scratch),
        compiler_params=pltpu.CompilerParams(vmem_limit_bytes=limit << 20),
        cost_estimate=pl.CostEstimate(flops=int(flops), bytes_accessed=int(moved), transcendentals=0),
        **options,
    )


def body(mlp_input, out_cot, w_in, w_out, chan_weights, row_weights, basis_spectra, band_cols, band_widths):
    tokens_n = ROWS * LONS
    depth = lax.axis_size("z")
    n_lat = depth * lax.axis_size("core")
    part = 640 // n_lat
    lat, lon, core = lax.axis_index(LAT), lax.axis_index(LON), lax.axis_index("core")
    tokens = mlp_input.transpose(1, 0, 2).reshape(tokens_n, 640)
    cotangent = out_cot.transpose(1, 0, 2).reshape(tokens_n, 640)
    whole = lambda *dims: pl.BlockSpec(dims, lambda i: (0,) * len(dims))

    half = shape(depth, 2, part, 1280)
    half_spec = pl.BlockSpec((depth, 2, part, 256), lambda i: (0, 0, 0, i))
    pre_grad, mine, theirs = call(
        head_kernel,
        (shape(tokens_n, 1280), half, half),
        None,
        3e9,
        8e6,
        [pltpu.VMEM((640, tokens_n), bf16), pltpu.VMEM((640, tokens_n), bf16), pltpu.VMEM((2, 640, 256), f32)],
        limit=62,
        grid=(5,),
        in_specs=[
            SMEM,
            whole(tokens_n, 640),
            whole(tokens_n, 640),
            pl.BlockSpec((640, 256), lambda i: (0, i)),
            pl.BlockSpec((256, 640), lambda i: (i, 0)),
        ],
        out_specs=[pl.BlockSpec((tokens_n, 256), lambda i: (0, i)), half_spec, half_spec],
    )(core.reshape(1), tokens, cotangent, w_in, w_out)
    partner = lax.ppermute(theirs, "core", [(0, 1), (1, 0)])

    send = call(
        lift_kernel,
        shape(PEERS, PAD, 128),
        None,
        2e9,
        4e6,
        [pltpu.VMEM((TALL, 128), f32)],
        limit=62,
        grid=(GROUPS,),
        in_specs=[
            whole(tokens_n, 1280),
            pl.BlockSpec((tokens_n, 128), lambda j: (0, j)),
            pl.BlockSpec((128, 1280), lambda j: (j, 0)),
        ],
        out_specs=whole(PEERS, PAD, 128),
    )(pre_grad, cotangent, w_in)
    received = lax.all_to_all(send, LON, split_axis=0, concat_axis=0, tiled=True)

    chip = (mine.astype(f32) + partner.astype(f32)).astype(bf16)
    column = lax.psum_scatter(chip, "z", scatter_dimension=0, tiled=True)

    own_mix, rim_mix, spread, ready = call(
        prep_kernel,
        (shape(GROUPS, NB * 128, 128), shape(NB * 256, 640), shape(NB, NLON, 128, dtype=f32), TOKEN),
        [SMEM] + [VMEM] * 5,
        1e9,
        6e6,
    )(
        jnp.stack([lat * ROWS, lon]).astype(jnp.int32),
        row_weights.transpose(0, 2, 1),
        band_cols.T,
        band_widths.reshape(1, -1),
        chan_weights,
        basis_spectra,
    )

    forward, inverse = tables()
    moved, first, last = call(
        open_kernel,
        (shape(NLON, 640), shape(NLON, 128), shape(NLON, 128)),
        [VMEM] * 3,
        1e8,
        2e6,
        [pltpu.VMEM((TALL, 128), f32)],
    )(received, rim_picks(), ready)
    up = [(i, i + 1) for i in range(n_lat - 1)]
    before = lax.ppermute(last, LAT, up)
    after = lax.ppermute(first, LAT, [(b, a) for a, b in up])

    filtered = call(
        own_kernel,
        shape(NLON, 640, dtype=f32),
        None,
        8e8,
        5e6,
        [pltpu.VMEM((NLON, NB * 128), bf16)],
        grid=(GROUPS,),
        in_specs=[
            pl.BlockSpec((NLON, 128), lambda j: (0, j)),
            whole(NLON, NLON),
            whole(NB, NLON, 128),
            pl.BlockSpec((1, NB * 128, 128), lambda j: (j, 0, 0)),
        ],
        out_specs=pl.BlockSpec((NLON, 128), lambda j: (0, j)),
    )(moved, forward, spread, own_mix)

    answer = call(
        close_kernel,
        shape(PEERS, PAD, 128),
        [VMEM] * 7,
        1.5e9,
        7e6,
        [pltpu.VMEM((NLON, NB * 256), bf16), pltpu.VMEM((TALL, 128), f32)],
    )(filtered, before, after, forward, inverse, spread, rim_mix)
    tall = PAD + 40 * -(-2 * part // 128)
    merged = call(merge_kernel, shape(PEERS, tall, 128), [VMEM] * 2, 1e6, 2e6, limit=62)(answer, column)
    returned = lax.all_to_all(merged, LON, split_axis=0, concat_axis=0, tiled=True)
    grid_grad, grad_in, grad_out = call(
        final_kernel,
        (shape(tokens_n, 640), shape(part, 40, dtype=f32), shape(40, part, dtype=f32)),
        [VMEM] * 2,
        1e8,
        2e6,
        [pltpu.VMEM((TALL, 128), f32)],
    )(returned, cotangent)
    grid_grad = grid_grad.reshape(LONS, ROWS, 640).transpose(1, 0, 2)
    return grid_grad, grad_in, grad_out


def solution(mesh):
    chips = Mesh(mesh.devices.reshape(-1, 2, 8, 4), ("z", "core", "y", "x"))
    grid = P(LAT, LON, None)
    return jax.shard_map(
        body,
        mesh=chips,
        in_specs=(grid, grid, P(), P(), P(), P(), P(), P(), P()),
        out_specs=(grid, P(LAT, LON), P(LON, LAT)),
        check_vma=False,
    )
```

```python
import functools
import math

import jax
import jax.numpy as jnp
import numpy as np
from jax import lax
from jax.experimental import pallas as pl
from jax.experimental.pallas import tpu as pltpu
from jax.sharding import Mesh, PartitionSpec as P

f32 = jnp.float32
bf16 = jnp.bfloat16
LAT = ("z", "core")
LON = ("y", "x")
ROWS = 32
LONS = 12
PEERS = 32
LOCAL = 20
NLON = 384
NF = 192
NB = 9
REACH = 4
GROUPS = 5
SLAB = LONS * GROUPS
PAD = 64
TALL = PEERS * SLAB + 8


def nt(a, b, precision=None):
    return lax.dot_general(a, b, (((1,), (1,)), ((), ())), preferred_element_type=f32, precision=precision)


def tn(a, b):
    return lax.dot_general(a, b, (((0,), (0,)), ((), ())), preferred_element_type=f32)


def nn(a, b, precision=None):
    return lax.dot_general(a, b, (((1,), (0,)), ((), ())), preferred_element_type=f32, precision=precision)


def swap_quarters(tiles):
    quarter = lax.broadcasted_iota(jnp.int32, tiles[0].shape, 1) // 32
    out = []
    for b in range(4):
        made = None
        for q in range(4):
            shift = (32 * (q - b)) % 128
            moved = pltpu.roll(tiles[q], shift, 1) if shift else tiles[q]
            made = moved if made is None else jnp.where(quarter == q, moved, made)
        out.append(made)
    return out


def gelu_parts(v):
    square = v * v
    tangent = jnp.tanh(0.7978845608 * (v + 0.044715 * v * square))
    half = 0.5 * (1.0 + tangent)
    slope = half + 0.5 * v * (1.0 - tangent * tangent) * 0.7978845608 * (1.0 + 0.134145 * square)
    return v * half, slope


def to_slabs(tall, out):
    for d in range(PEERS):
        out[d] = tall[SLAB * d : SLAB * d + PAD, :].astype(bf16)


def from_slabs(slabs, tall):
    for d in range(PEERS):
        tall[SLAB * d : SLAB * d + PAD, :] = slabs[d].astype(f32)


def head_kernel(core, tok, cot, w_in, w_out, pre_grad, mine, theirs, tok_t, cot_t, scr):
    @pl.when(pl.program_id(0) == 0)
    def _():
        tok_t[...] = tok[...].astype(f32).T.astype(bf16)
        cot_t[...] = cot[...].astype(f32).T.astype(bf16)

    gelu_value, slope = gelu_parts(nn(tok[...], w_in[...]))
    grad = (nt(cot[...], w_out[...]) * slope).astype(bf16)
    pre_grad[...] = grad
    c = core[0]
    depth, _, size = mine.shape[0], mine.shape[1], mine.shape[2]
    for which, (left, right) in enumerate(((tok_t, grad), (cot_t, gelu_value.astype(bf16)))):
        scr[which] = nn(left[...], right)
        for z in range(depth):
            own = pl.multiple_of((2 * z + c) * size, 8)
            other = pl.multiple_of((2 * z + 1 - c) * size, 8)
            mine[z, which] = scr[which, pl.ds(own, size), :].astype(bf16)
            theirs[z, which] = scr[which, pl.ds(other, size), :].astype(bf16)


def lift_kernel(pre_grad, cot, w_in, send, tall):
    j = pl.program_id(0)
    whole = cot[...].astype(f32).T + nt(w_in[...], pre_grad[...])
    for a in range(LONS // 4):
        tiles = [whole[q * 32 : (q + 1) * 32, a * 128 : (a + 1) * 128] for q in range(4)]
        for b, tile in enumerate(swap_quarters(tiles)):
            tall[pl.ds((4 * a + b) * GROUPS + j, PEERS, stride=SLAB), :] = tile

    @pl.when(j == pl.num_programs(0) - 1)
    def _():
        tall[TALL - 8 :, :] = jnp.zeros((8, 128), f32)
        to_slabs(tall, send)


def prep_kernel(place, row_w, cols, widths, chan, basis, own_mix, rim_mix, spread, token):
    token[...] = jnp.zeros(token.shape, f32)
    row_start, lon = place[0], place[1]
    high = lax.Precision.HIGHEST
    count = cols.shape[1]
    at = lax.broadcasted_iota(jnp.int32, (64, count), 0)
    rim = at % 4
    source = jnp.where(at < 32, at, jnp.where(at < 48, rim - REACH, rim + ROWS)) + row_start
    pick = (source == lax.broadcasted_iota(jnp.int32, (64, count), 1)).astype(f32)
    col = nt(pick, cols[...].astype(f32), high) - row_start.astype(f32)
    width = nt(pick, widths[...].astype(f32), high)
    lane = lax.broadcasted_iota(jnp.int32, (64, 128), 1)
    target = (lane % 32).astype(f32)
    hits = [
        jnp.where((col[:, s : s + 1] == target) & (width > s), 1.0, 0.0) for s in range(NB)
    ]
    chan_row = lax.broadcasted_iota(jnp.int32, (640, 640), 0)
    chan_lane = lax.broadcasted_iota(jnp.int32, (640, 640), 1)
    chan_pick = (chan_row == (chan_lane // 32) * 32 + lon).astype(f32)
    chan_w = nn(chan[...], chan_pick, high)
    rim_mix[...] = jnp.zeros(rim_mix.shape, bf16)
    quarter = lane[:32] // 32
    rim_at = lax.broadcasted_iota(jnp.int32, (16, 128), 0) // 4
    rim_quarter = lane[:16] // 32
    for k in range(NB):
        coef = nt(pick, row_w[k], high)
        weight = None
        for s in range(NB):
            term = coef[:, s : s + 1] * hits[s]
            weight = term if weight is None else weight + term
        for j in range(GROUPS):
            scaled = weight * chan_w[k : k + 1, 128 * j : 128 * (j + 1)]
            for q in range(4):
                own_mix[j, k * 128 + q * 32 : k * 128 + (q + 1) * 32, :] = jnp.where(
                    quarter == q, scaled[:32], 0.0
                ).astype(bf16)
            for side in range(2):
                part = scaled[32 + 16 * side : 48 + 16 * side]
                start = (k * 2 + side) * 128 + 16 * j
                rim_mix[start : start + 16, 128 * j : 128 * (j + 1)] = jnp.where(
                    rim_quarter == rim_at, part, 0.0
                ).astype(bf16)
        spread[k] = jnp.broadcast_to(basis[k : k + 1, :], (128, NLON)).T


def open_kernel(slabs, pick, _ready, moved, first, last, tall):
    from_slabs(slabs, tall)
    for j in range(GROUPS):
        moved[:, 128 * j : 128 * (j + 1)] = tall[pl.ds(j, NLON, stride=GROUPS), :].astype(bf16)
    edges = nn(moved[...], pick[...]).astype(bf16)
    last[...] = edges[:, :128]
    first[...] = edges[:, 128:]


def own_kernel(moved, forward, spread, own_mix, filtered, mixed):
    spectra = nn(forward[...], moved[...])
    first, second = spectra[:NF], spectra[NF:]
    for k in range(NB):
        cosine, sine = spread[k, :NF], spread[k, NF:]
        mixed[:NF, k * 128 : (k + 1) * 128] = (cosine * first + sine * second).astype(bf16)
        mixed[NF:, k * 128 : (k + 1) * 128] = (cosine * second - sine * first).astype(bf16)
    filtered[...] = nn(mixed[...], own_mix[0])


def close_kernel(filtered, before, after, forward, inverse, spread, rim_mix, send, mixed, tall):
    for side, rim in enumerate((before, after)):
        spectra = nn(forward[...], rim[...])
        first, second = spectra[:NF], spectra[NF:]
        for k in range(NB):
            cosine, sine = spread[k, :NF], spread[k, NF:]
            at = (k * 2 + side) * 128
            mixed[:NF, at : at + 128] = (cosine * first + sine * second).astype(bf16)
            mixed[NF:, at : at + 128] = (cosine * second - sine * first).astype(bf16)
    whole = (filtered[...] + nn(mixed[...], rim_mix[...])).astype(bf16)
    tall[TALL - 8 :, :] = jnp.zeros((8, 128), f32)
    for j in range(GROUPS):
        tall[pl.ds(j, NLON, stride=GROUPS), :] = nn(inverse[...], whole[:, 128 * j : 128 * (j + 1)])
    to_slabs(tall, send)


def merge_kernel(answer, column, out):
    rows = column[0, 0].astype(f32), column[0, 1].astype(f32)
    fill = jnp.zeros((-(2 * rows[0].shape[0]) % 128, rows[0].shape[1]), f32)
    turned = jnp.concatenate([rows[0], rows[1], fill], 0).T
    for d in range(PEERS):
        out[d, :PAD] = answer[d]
        for i in range(turned.shape[1] // 128):
            out[d, PAD + 40 * i : PAD + 40 * (i + 1)] = turned[40 * d : 40 * (d + 1), 128 * i : 128 * (i + 1)].astype(bf16)


def final_kernel(slabs, cot, out, grad_in, grad_out, tall):
    for d in range(PEERS):
        tall[SLAB * d : SLAB * d + PAD, :] = slabs[d, :PAD].astype(f32)
    for j in range(GROUPS):
        for a in range(LONS // 4):
            tiles = [tall[pl.ds((4 * a + b) * GROUPS + j, PEERS, stride=SLAB), :] for b in range(4)]
            turned = jnp.concatenate(tiles, 0).T
            for b, tile in enumerate(swap_quarters([turned[32 * q : 32 * (q + 1)] for q in range(4)])):
                rows = slice((4 * a + b) * 32, (4 * a + b + 1) * 32)
                lanes = slice(128 * j, 128 * (j + 1))
                out[rows, lanes] = (cot[rows, lanes].astype(f32) + tile).astype(bf16)
    size = grad_in.shape[0]
    total = slabs[0, PAD:].astype(f32)
    for d in range(1, PEERS):
        total = total + slabs[d, PAD:].astype(f32)
    if total.shape[0] > 40:
        total = jnp.concatenate([total[i : i + 40] for i in range(0, total.shape[0], 40)], 1)
    lanes = total.shape[1]
    filled = jnp.concatenate([total, jnp.zeros((128 - 40, lanes), f32)], 0)
    grad_in[...] = filled.T[:size, :40]
    grad_out[...] = total[:, size : 2 * size]


def tables():
    lon = np.arange(NLON)
    freq = np.arange(NLON) % NF
    phase = (lon[:, None] * freq[None, :] % NLON) * (2.0 * math.pi / NLON)
    forward = np.where(np.arange(NLON)[None, :] >= NF, np.sin(phase), np.cos(phase))
    inverse = forward.T * (np.where(freq == 0, 1.0, 2.0) / NLON)[:, None]
    return jnp.asarray(forward.T, bf16), jnp.asarray(inverse.T, bf16)


def rim_picks():
    pick = np.zeros((640, 256), np.float32)
    for c in range(LOCAL):
        for r in range(REACH):
            pick[c * 32 + ROWS - REACH + r, c * 4 + r] = 1.0
            pick[c * 32 + r, 128 + c * 4 + r] = 1.0
    return jnp.asarray(pick, bf16)


def shape(*dims, dtype=bf16):
    return jax.ShapeDtypeStruct(dims, dtype)


VMEM = pl.BlockSpec(memory_space=pltpu.VMEM)
TOKEN = shape(8, 128, dtype=f32)
SMEM = pl.BlockSpec(memory_space=pltpu.SMEM)


def call(kernel, out, ins, flops, moved, scratch=(), limit=24, **grid):
    options = dict(grid)
    if "grid" not in options:
        options["in_specs"] = ins
        options["out_specs"] = jax.tree.map(lambda _: VMEM, out)
    return pl.pallas_call(
        kernel,
        out_shape=out,
        scratch_shapes=list(scratch),
        compiler_params=pltpu.CompilerParams(vmem_limit_bytes=limit << 20),
        cost_estimate=pl.CostEstimate(flops=int(flops), bytes_accessed=int(moved), transcendentals=0),
        **options,
    )


def body(mlp_input, out_cot, w_in, w_out, chan_weights, row_weights, basis_spectra, band_cols, band_widths):
    tokens_n = ROWS * LONS
    depth = lax.axis_size("z")
    n_lat = depth * lax.axis_size("core")
    part = 640 // n_lat
    lat, lon, core = lax.axis_index(LAT), lax.axis_index(LON), lax.axis_index("core")
    tokens = mlp_input.transpose(1, 0, 2).reshape(tokens_n, 640)
    cotangent = out_cot.transpose(1, 0, 2).reshape(tokens_n, 640)
    whole = lambda *dims: pl.BlockSpec(dims, lambda i: (0,) * len(dims))

    half = shape(depth, 2, part, 1280)
    half_spec = pl.BlockSpec((depth, 2, part, 256), lambda i: (0, 0, 0, i))
    pre_grad, mine, theirs = call(
        head_kernel,
        (shape(tokens_n, 1280), half, half),
        None,
        3e9,
        8e6,
        [pltpu.VMEM((640, tokens_n), bf16), pltpu.VMEM((640, tokens_n), bf16), pltpu.VMEM((2, 640, 256), f32)],
        limit=48,
        grid=(5,),
        in_specs=[
            SMEM,
            whole(tokens_n, 640),
            whole(tokens_n, 640),
            pl.BlockSpec((640, 256), lambda i: (0, i)),
            pl.BlockSpec((256, 640), lambda i: (i, 0)),
        ],
        out_specs=[pl.BlockSpec((tokens_n, 256), lambda i: (0, i)), half_spec, half_spec],
    )(core.reshape(1), tokens, cotangent, w_in, w_out)
    partner = lax.ppermute(theirs, "core", [(0, 1), (1, 0)])

    send = call(
        lift_kernel,
        shape(PEERS, PAD, 128),
        None,
        2e9,
        4e6,
        [pltpu.VMEM((TALL, 128), f32)],
        limit=48,
        grid=(GROUPS,),
        in_specs=[
            whole(tokens_n, 1280),
            pl.BlockSpec((tokens_n, 128), lambda j: (0, j)),
            pl.BlockSpec((128, 1280), lambda j: (j, 0)),
        ],
        out_specs=whole(PEERS, PAD, 128),
    )(pre_grad, cotangent, w_in)
    received = lax.all_to_all(send, LON, split_axis=0, concat_axis=0, tiled=True)

    mine, send = lax.optimization_barrier((mine, send))
    chip = (mine.astype(f32) + partner.astype(f32)).astype(bf16)
    column = lax.psum_scatter(chip, "z", scatter_dimension=0, tiled=True)

    own_mix, rim_mix, spread, ready = call(
        prep_kernel,
        (shape(GROUPS, NB * 128, 128), shape(NB * 256, 640), shape(NB, NLON, 128, dtype=f32), TOKEN),
        [SMEM] + [VMEM] * 5,
        1e9,
        6e6,
    )(
        jnp.stack([lat * ROWS, lon]).astype(jnp.int32),
        row_weights.transpose(0, 2, 1),
        band_cols.T,
        band_widths.reshape(1, -1),
        chan_weights,
        basis_spectra,
    )

    forward, inverse = tables()
    moved, first, last = call(
        open_kernel,
        (shape(NLON, 640), shape(NLON, 128), shape(NLON, 128)),
        [VMEM] * 3,
        1e8,
        2e6,
        [pltpu.VMEM((TALL, 128), f32)],
    )(received, rim_picks(), ready)
    up = [(i, i + 1) for i in range(n_lat - 1)]
    before = lax.ppermute(last, LAT, up)
    after = lax.ppermute(first, LAT, [(b, a) for a, b in up])

    filtered = call(
        own_kernel,
        shape(NLON, 640, dtype=f32),
        None,
        8e8,
        5e6,
        [pltpu.VMEM((NLON, NB * 128), bf16)],
        grid=(GROUPS,),
        in_specs=[
            pl.BlockSpec((NLON, 128), lambda j: (0, j)),
            whole(NLON, NLON),
            whole(NB, NLON, 128),
            pl.BlockSpec((1, NB * 128, 128), lambda j: (j, 0, 0)),
        ],
        out_specs=pl.BlockSpec((NLON, 128), lambda j: (0, j)),
    )(moved, forward, spread, own_mix)

    answer = call(
        close_kernel,
        shape(PEERS, PAD, 128),
        [VMEM] * 7,
        1.5e9,
        7e6,
        [pltpu.VMEM((NLON, NB * 256), bf16), pltpu.VMEM((TALL, 128), f32)],
    )(filtered, before, after, forward, inverse, spread, rim_mix)
    tall = PAD + 40 * -(-2 * part // 128)
    merged = call(merge_kernel, shape(PEERS, tall, 128), [VMEM] * 2, 1e6, 2e6, limit=62)(answer, column)
    returned = lax.all_to_all(merged, LON, split_axis=0, concat_axis=0, tiled=True)
    grid_grad, grad_in, grad_out = call(
        final_kernel,
        (shape(tokens_n, 640), shape(part, 40, dtype=f32), shape(40, part, dtype=f32)),
        [VMEM] * 2,
        1e8,
        2e6,
        [pltpu.VMEM((TALL, 128), f32)],
    )(returned, cotangent)
    grid_grad = grid_grad.reshape(LONS, ROWS, 640).transpose(1, 0, 2)
    return grid_grad, grad_in, grad_out


def solution(mesh):
    chips = Mesh(mesh.devices.reshape(-1, 2, 8, 4), ("z", "core", "y", "x"))
    grid = P(LAT, LON, None)
    return jax.shard_map(
        body,
        mesh=chips,
        in_specs=(grid, grid, P(), P(), P(), P(), P(), P(), P()),
        out_specs=(grid, P(LAT, LON), P(LON, LAT)),
        check_vma=False,
    )
```

```python
import functools
import math

import jax
import jax.numpy as jnp
import numpy as np
from jax import lax
from jax.experimental import pallas as pl
from jax.experimental.pallas import tpu as pltpu
from jax.sharding import Mesh, PartitionSpec as P

f32 = jnp.float32
bf16 = jnp.bfloat16
LAT = ("z", "core")
LON = ("y", "x")
ROWS = 32
LONS = 12
PEERS = 32
LOCAL = 20
NLON = 384
NF = 192
NB = 9
REACH = 4
GROUPS = 5
SLAB = LONS * GROUPS
PAD = 64
TALL = PEERS * SLAB + 8


def nt(a, b, precision=None):
    return lax.dot_general(a, b, (((1,), (1,)), ((), ())), preferred_element_type=f32, precision=precision)


def tn(a, b):
    return lax.dot_general(a, b, (((0,), (0,)), ((), ())), preferred_element_type=f32)


def nn(a, b, precision=None):
    return lax.dot_general(a, b, (((1,), (0,)), ((), ())), preferred_element_type=f32, precision=precision)


def swap_quarters(tiles):
    quarter = lax.broadcasted_iota(jnp.int32, tiles[0].shape, 1) // 32
    out = []
    for b in range(4):
        made = None
        for q in range(4):
            shift = (32 * (q - b)) % 128
            moved = pltpu.roll(tiles[q], shift, 1) if shift else tiles[q]
            made = moved if made is None else jnp.where(quarter == q, moved, made)
        out.append(made)
    return out


def gelu_parts(v):
    square = v * v
    tangent = jnp.tanh(0.7978845608 * (v + 0.044715 * v * square))
    half = 0.5 * (1.0 + tangent)
    slope = half + 0.5 * v * (1.0 - tangent * tangent) * 0.7978845608 * (1.0 + 0.134145 * square)
    return v * half, slope


def to_slabs(tall, out):
    for d in range(PEERS):
        out[d] = tall[SLAB * d : SLAB * d + PAD, :].astype(bf16)


def from_slabs(slabs, tall):
    for d in range(PEERS):
        tall[SLAB * d : SLAB * d + PAD, :] = slabs[d].astype(f32)


def head_kernel(core, tok, cot, w_in, w_out, pre_grad, mine, theirs, tok_t, cot_t, scr):
    @pl.when(pl.program_id(0) == 0)
    def _():
        tok_t[...] = tok[...].astype(f32).T.astype(bf16)
        cot_t[...] = cot[...].astype(f32).T.astype(bf16)

    gelu_value, slope = gelu_parts(nn(tok[...], w_in[...]))
    grad = (nt(cot[...], w_out[...]) * slope).astype(bf16)
    pre_grad[...] = grad
    c = core[0]
    depth, _, size = mine.shape[0], mine.shape[1], mine.shape[2]
    for which, (left, right) in enumerate(((tok_t, grad), (cot_t, gelu_value.astype(bf16)))):
        scr[which] = nn(left[...], right)
        for z in range(depth):
            own = pl.multiple_of((2 * z + c) * size, 8)
            other = pl.multiple_of((2 * z + 1 - c) * size, 8)
            mine[z, which] = scr[which, pl.ds(own, size), :].astype(bf16)
            theirs[z, which] = scr[which, pl.ds(other, size), :].astype(bf16)


def lift_kernel(pre_grad, cot, w_in, send, tall):
    j = pl.program_id(0)
    whole = cot[...].astype(f32).T + nt(w_in[...], pre_grad[...])
    for a in range(LONS // 4):
        tiles = [whole[q * 32 : (q + 1) * 32, a * 128 : (a + 1) * 128] for q in range(4)]
        for b, tile in enumerate(swap_quarters(tiles)):
            tall[pl.ds((4 * a + b) * GROUPS + j, PEERS, stride=SLAB), :] = tile

    @pl.when(j == pl.num_programs(0) - 1)
    def _():
        tall[TALL - 8 :, :] = jnp.zeros((8, 128), f32)
        to_slabs(tall, send)


def prep_kernel(place, row_w, cols, widths, chan, basis, own_mix, rim_mix, spread, token):
    token[...] = jnp.zeros(token.shape, f32)
    row_start, lon = place[0], place[1]
    high = lax.Precision.HIGHEST
    count = cols.shape[1]
    at = lax.broadcasted_iota(jnp.int32, (64, count), 0)
    rim = at % 4
    source = jnp.where(at < 32, at, jnp.where(at < 48, rim - REACH, rim + ROWS)) + row_start
    pick = (source == lax.broadcasted_iota(jnp.int32, (64, count), 1)).astype(f32)
    col = nt(pick, cols[...].astype(f32), high) - row_start.astype(f32)
    width = nt(pick, widths[...].astype(f32), high)
    lane = lax.broadcasted_iota(jnp.int32, (64, 128), 1)
    target = (lane % 32).astype(f32)
    hits = [
        jnp.where((col[:, s : s + 1] == target) & (width > s), 1.0, 0.0) for s in range(NB)
    ]
    chan_row = lax.broadcasted_iota(jnp.int32, (640, 640), 0)
    chan_lane = lax.broadcasted_iota(jnp.int32, (640, 640), 1)
    chan_pick = (chan_row == (chan_lane // 32) * 32 + lon).astype(f32)
    chan_w = nn(chan[...], chan_pick, high)
    rim_mix[...] = jnp.zeros(rim_mix.shape, bf16)
    quarter = lane[:32] // 32
    rim_at = lax.broadcasted_iota(jnp.int32, (16, 128), 0) // 4
    rim_quarter = lane[:16] // 32
    for k in range(NB):
        coef = nt(pick, row_w[k], high)
        weight = None
        for s in range(NB):
            term = coef[:, s : s + 1] * hits[s]
            weight = term if weight is None else weight + term
        for j in range(GROUPS):
            scaled = weight * chan_w[k : k + 1, 128 * j : 128 * (j + 1)]
            for q in range(4):
                own_mix[j, k * 128 + q * 32 : k * 128 + (q + 1) * 32, :] = jnp.where(
                    quarter == q, scaled[:32], 0.0
                ).astype(bf16)
            for side in range(2):
                part = scaled[32 + 16 * side : 48 + 16 * side]
                start = (k * 2 + side) * 128 + 16 * j
                rim_mix[start : start + 16, 128 * j : 128 * (j + 1)] = jnp.where(
                    rim_quarter == rim_at, part, 0.0
                ).astype(bf16)
        spread[k] = jnp.broadcast_to(basis[k : k + 1, :], (128, NLON)).T


def open_kernel(slabs, pick, _ready, moved, first, last, tall):
    from_slabs(slabs, tall)
    for j in range(GROUPS):
        moved[:, 128 * j : 128 * (j + 1)] = tall[pl.ds(j, NLON, stride=GROUPS), :].astype(bf16)
    edges = nn(moved[...], pick[...]).astype(bf16)
    last[...] = edges[:, :128]
    first[...] = edges[:, 128:]


def own_kernel(moved, forward, spread, own_mix, filtered, mixed):
    spectra = nn(forward[...], moved[...])
    first, second = spectra[:NF], spectra[NF:]
    for k in range(NB):
        cosine, sine = spread[k, :NF], spread[k, NF:]
        mixed[:NF, k * 128 : (k + 1) * 128] = (cosine * first + sine * second).astype(bf16)
        mixed[NF:, k * 128 : (k + 1) * 128] = (cosine * second - sine * first).astype(bf16)
    filtered[...] = nn(mixed[...], own_mix[0])


def close_kernel(filtered, before, after, forward, inverse, spread, rim_mix, send, mixed, tall):
    for side, rim in enumerate((before, after)):
        spectra = nn(forward[...], rim[...])
        first, second = spectra[:NF], spectra[NF:]
        for k in range(NB):
            cosine, sine = spread[k, :NF], spread[k, NF:]
            at = (k * 2 + side) * 128
            mixed[:NF, at : at + 128] = (cosine * first + sine * second).astype(bf16)
            mixed[NF:, at : at + 128] = (cosine * second - sine * first).astype(bf16)
    whole = (filtered[...] + nn(mixed[...], rim_mix[...])).astype(bf16)
    tall[TALL - 8 :, :] = jnp.zeros((8, 128), f32)
    for j in range(GROUPS):
        tall[pl.ds(j, NLON, stride=GROUPS), :] = nn(inverse[...], whole[:, 128 * j : 128 * (j + 1)])
    to_slabs(tall, send)


def merge_kernel(answer, column, out, piece, sem):
    rows = column[0, 0].astype(f32), column[0, 1].astype(f32)
    filled = 2 * rows[0].shape[0]
    fill = jnp.zeros((-filled % 128, rows[0].shape[1]), f32)
    turned = jnp.concatenate([rows[0], rows[1], fill], 0).T
    lane = lax.broadcasted_iota(jnp.int32, (8, 128), 1)
    for d in range(PEERS):
        own = turned[40 * d : 40 * (d + 1)]
        if filled == 80:
            end = own[32:]
            piece[d] = jnp.concatenate(
                [
                    own[:8] + pltpu.roll(jnp.where(lane < 48, end, 0.0), 80, 1),
                    own[8:16] + pltpu.roll(jnp.where(lane < 48, 0.0, end), 32, 1),
                    own[16:32],
                ],
                0,
            ).astype(bf16)
        else:
            for i in range(turned.shape[1] // 128):
                piece[d, 40 * i : 40 * (i + 1)] = own[:, 128 * i : 128 * (i + 1)].astype(bf16)
    copy = pltpu.make_async_copy(piece, out.at[:, PAD : PAD + piece.shape[1]], sem)
    copy.start()
    copy.wait()


def final_kernel(slabs, cot, out, grad_in, grad_out, tall):
    for d in range(PEERS):
        tall[SLAB * d : SLAB * d + PAD, :] = slabs[d, :PAD].astype(f32)
    for j in range(GROUPS):
        for a in range(LONS // 4):
            tiles = [tall[pl.ds((4 * a + b) * GROUPS + j, PEERS, stride=SLAB), :] for b in range(4)]
            turned = jnp.concatenate(tiles, 0).T
            for b, tile in enumerate(swap_quarters([turned[32 * q : 32 * (q + 1)] for q in range(4)])):
                rows = slice((4 * a + b) * 32, (4 * a + b + 1) * 32)
                lanes = slice(128 * j, 128 * (j + 1))
                out[rows, lanes] = (cot[rows, lanes].astype(f32) + tile).astype(bf16)
    size = grad_in.shape[0]
    total = slabs[0, PAD:].astype(f32)
    for d in range(1, PEERS):
        total = total + slabs[d, PAD:].astype(f32)
    if total.shape[0] == 32:
        lane = lax.broadcasted_iota(jnp.int32, (8, 128), 1)
        end = jnp.where(lane < 48, pltpu.roll(total[:8], 48, 1), pltpu.roll(total[8:16], 96, 1))
        total = jnp.concatenate([total, end], 0)
    elif total.shape[0] > 40:
        total = jnp.concatenate([total[i : i + 40] for i in range(0, total.shape[0], 40)], 1)
    lanes = total.shape[1]
    filled = jnp.concatenate([total, jnp.zeros((128 - 40, lanes), f32)], 0)
    grad_in[...] = filled.T[:size, :40]
    grad_out[...] = total[:, size : 2 * size]


def tables():
    lon = np.arange(NLON)
    freq = np.arange(NLON) % NF
    phase = (lon[:, None] * freq[None, :] % NLON) * (2.0 * math.pi / NLON)
    forward = np.where(np.arange(NLON)[None, :] >= NF, np.sin(phase), np.cos(phase))
    inverse = forward.T * (np.where(freq == 0, 1.0, 2.0) / NLON)[:, None]
    return jnp.asarray(forward.T, bf16), jnp.asarray(inverse.T, bf16)


def rim_picks():
    pick = np.zeros((640, 256), np.float32)
    for c in range(LOCAL):
        for r in range(REACH):
            pick[c * 32 + ROWS - REACH + r, c * 4 + r] = 1.0
            pick[c * 32 + r, 128 + c * 4 + r] = 1.0
    return jnp.asarray(pick, bf16)


def shape(*dims, dtype=bf16):
    return jax.ShapeDtypeStruct(dims, dtype)


VMEM = pl.BlockSpec(memory_space=pltpu.VMEM)
TOKEN = shape(8, 128, dtype=f32)
ANY = pl.BlockSpec(memory_space=pl.ANY)
SMEM = pl.BlockSpec(memory_space=pltpu.SMEM)


def call(kernel, out, ins, flops, moved, scratch=(), limit=24, **grid):
    options = dict(grid)
    if "grid" not in options:
        options["in_specs"] = ins
        options.setdefault("out_specs", jax.tree.map(lambda _: VMEM, out))
    return pl.pallas_call(
        kernel,
        out_shape=out,
        scratch_shapes=list(scratch),
        compiler_params=pltpu.CompilerParams(vmem_limit_bytes=limit << 20),
        cost_estimate=pl.CostEstimate(flops=int(flops), bytes_accessed=int(moved), transcendentals=0),
        **options,
    )


def body(mlp_input, out_cot, w_in, w_out, chan_weights, row_weights, basis_spectra, band_cols, band_widths):
    tokens_n = ROWS * LONS
    depth = lax.axis_size("z")
    n_lat = depth * lax.axis_size("core")
    part = 640 // n_lat
    lat, lon, core = lax.axis_index(LAT), lax.axis_index(LON), lax.axis_index("core")
    tokens = mlp_input.transpose(1, 0, 2).reshape(tokens_n, 640)
    cotangent = out_cot.transpose(1, 0, 2).reshape(tokens_n, 640)
    whole = lambda *dims: pl.BlockSpec(dims, lambda i: (0,) * len(dims))

    half = shape(depth, 2, part, 1280)
    half_spec = pl.BlockSpec((depth, 2, part, 640), lambda i: (0, 0, 0, i))
    pre_grad, mine, theirs = call(
        head_kernel,
        (shape(tokens_n, 1280), half, half),
        None,
        3e9,
        8e6,
        [pltpu.VMEM((640, tokens_n), bf16), pltpu.VMEM((640, tokens_n), bf16), pltpu.VMEM((2, 640, 640), f32)],
        limit=48,
        grid=(2,),
        in_specs=[
            SMEM,
            whole(tokens_n, 640),
            whole(tokens_n, 640),
            pl.BlockSpec((640, 640), lambda i: (0, i)),
            pl.BlockSpec((640, 640), lambda i: (i, 0)),
        ],
        out_specs=[pl.BlockSpec((tokens_n, 640), lambda i: (0, i)), half_spec, half_spec],
    )(core.reshape(1), tokens, cotangent, w_in, w_out)
    partner = lax.ppermute(theirs, "core", [(0, 1), (1, 0)])

    send = call(
        lift_kernel,
        shape(PEERS, PAD, 128),
        None,
        2e9,
        4e6,
        [pltpu.VMEM((TALL, 128), f32)],
        limit=48,
        grid=(GROUPS,),
        in_specs=[
            whole(tokens_n, 1280),
            pl.BlockSpec((tokens_n, 128), lambda j: (0, j)),
            pl.BlockSpec((128, 1280), lambda j: (j, 0)),
        ],
        out_specs=whole(PEERS, PAD, 128),
    )(pre_grad, cotangent, w_in)
    received = lax.all_to_all(send, LON, split_axis=0, concat_axis=0, tiled=True)

    mine, send = lax.optimization_barrier((mine, send))
    chip = (mine.astype(f32) + partner.astype(f32)).astype(bf16)
    column = lax.psum_scatter(chip, "z", scatter_dimension=0, tiled=True)

    own_mix, rim_mix, spread, ready = call(
        prep_kernel,
        (shape(GROUPS, NB * 128, 128), shape(NB * 256, 640), shape(NB, NLON, 128, dtype=f32), TOKEN),
        [SMEM] + [VMEM] * 5,
        1e9,
        6e6,
    )(
        jnp.stack([lat * ROWS, lon]).astype(jnp.int32),
        row_weights.transpose(0, 2, 1),
        band_cols.T,
        band_widths.reshape(1, -1),
        chan_weights,
        basis_spectra,
    )

    forward, inverse = tables()
    moved, first, last = call(
        open_kernel,
        (shape(NLON, 640), shape(NLON, 128), shape(NLON, 128)),
        [VMEM] * 3,
        1e8,
        2e6,
        [pltpu.VMEM((TALL, 128), f32)],
    )(received, rim_picks(), ready)
    up = [(i, i + 1) for i in range(n_lat - 1)]
    before = lax.ppermute(last, LAT, up)
    after = lax.ppermute(first, LAT, [(b, a) for a, b in up])

    filtered = call(
        own_kernel,
        shape(NLON, 640, dtype=f32),
        None,
        8e8,
        5e6,
        [pltpu.VMEM((NLON, NB * 128), bf16)],
        grid=(GROUPS,),
        in_specs=[
            pl.BlockSpec((NLON, 128), lambda j: (0, j)),
            whole(NLON, NLON),
            whole(NB, NLON, 128),
            pl.BlockSpec((1, NB * 128, 128), lambda j: (j, 0, 0)),
        ],
        out_specs=pl.BlockSpec((NLON, 128), lambda j: (0, j)),
    )(moved, forward, spread, own_mix)

    extra = 32 if part == 40 else 40 * -(-2 * part // 128)
    answer = call(
        close_kernel,
        shape(PEERS, PAD + extra, 128),
        None,
        1.5e9,
        7e6,
        [pltpu.VMEM((NLON, NB * 256), bf16), pltpu.VMEM((TALL, 128), f32)],
        grid=(1,),
        in_specs=[VMEM] * 7,
        out_specs=whole(PEERS, PAD, 128),
    )(filtered, before, after, forward, inverse, spread, rim_mix)
    merged = call(
        merge_kernel,
        shape(PEERS, PAD + extra, 128),
        [ANY, VMEM],
        1e6,
        2e6,
        [pltpu.VMEM((PEERS, extra, 128), bf16), pltpu.SemaphoreType.DMA],
        out_specs=ANY,
        input_output_aliases={0: 0},
    )(answer, column)
    returned = lax.all_to_all(merged, LON, split_axis=0, concat_axis=0, tiled=True)
    grid_grad, grad_in, grad_out = call(
        final_kernel,
        (shape(tokens_n, 640), shape(part, 40, dtype=f32), shape(40, part, dtype=f32)),
        [VMEM] * 2,
        1e8,
        2e6,
        [pltpu.VMEM((TALL, 128), f32)],
    )(returned, cotangent)
    grid_grad = grid_grad.reshape(LONS, ROWS, 640).transpose(1, 0, 2)
    return grid_grad, grad_in, grad_out


def solution(mesh):
    chips = Mesh(mesh.devices.reshape(-1, 2, 8, 4), ("z", "core", "y", "x"))
    grid = P(LAT, LON, None)
    return jax.shard_map(
        body,
        mesh=chips,
        in_specs=(grid, grid, P(), P(), P(), P(), P(), P(), P()),
        out_specs=(grid, P(LAT, LON), P(LON, LAT)),
        check_vma=False,
    )
```

```python
import functools
import math

import jax
import jax.numpy as jnp
import numpy as np
from jax import lax
from jax.experimental import pallas as pl
from jax.experimental.pallas import tpu as pltpu
from jax.sharding import Mesh, PartitionSpec as P

f32 = jnp.float32
bf16 = jnp.bfloat16
LAT = ("z", "core")
LON = ("y", "x")
ROWS = 32
LONS = 12
PEERS = 32
LOCAL = 20
NLON = 384
NF = 192
NB = 9
REACH = 4
GROUPS = 5
SLAB = LONS * GROUPS
PAD = 64
TALL = PEERS * SLAB + 8


def nt(a, b, precision=None):
    return lax.dot_general(a, b, (((1,), (1,)), ((), ())), preferred_element_type=f32, precision=precision)


def tn(a, b):
    return lax.dot_general(a, b, (((0,), (0,)), ((), ())), preferred_element_type=f32)


def nn(a, b, precision=None):
    return lax.dot_general(a, b, (((1,), (0,)), ((), ())), preferred_element_type=f32, precision=precision)


def swap_quarters(tiles):
    quarter = lax.broadcasted_iota(jnp.int32, tiles[0].shape, 1) // 32
    out = []
    for b in range(4):
        made = None
        for q in range(4):
            shift = (32 * (q - b)) % 128
            moved = pltpu.roll(tiles[q], shift, 1) if shift else tiles[q]
            made = moved if made is None else jnp.where(quarter == q, moved, made)
        out.append(made)
    return out


def gelu_parts(v):
    square = v * v
    tangent = jnp.tanh(0.7978845608 * (v + 0.044715 * v * square))
    half = 0.5 * (1.0 + tangent)
    slope = half + 0.5 * v * (1.0 - tangent * tangent) * 0.7978845608 * (1.0 + 0.134145 * square)
    return v * half, slope


def to_slabs(tall, out):
    for d in range(PEERS):
        out[d] = tall[SLAB * d : SLAB * d + PAD, :].astype(bf16)


def from_slabs(slabs, tall):
    for d in range(PEERS):
        tall[SLAB * d : SLAB * d + PAD, :] = slabs[d].astype(f32)


def head_kernel(core, tok, cot, w_in, w_out, pre_grad, mine, theirs, tok_t, cot_t, scr):
    @pl.when(pl.program_id(0) == 0)
    def _():
        tok_t[...] = tok[...].astype(f32).T.astype(bf16)
        cot_t[...] = cot[...].astype(f32).T.astype(bf16)

    gelu_value, slope = gelu_parts(nn(tok[...], w_in[...]))
    grad = (nt(cot[...], w_out[...]) * slope).astype(bf16)
    pre_grad[...] = grad
    c = core[0]
    depth, _, size = mine.shape[0], mine.shape[1], mine.shape[2]
    for which, (left, right) in enumerate(((tok_t, grad), (cot_t, gelu_value.astype(bf16)))):
        scr[which] = nn(left[...], right)
        for z in range(depth):
            own = pl.multiple_of((2 * z + c) * size, 8)
            other = pl.multiple_of((2 * z + 1 - c) * size, 8)
            mine[z, which] = scr[which, pl.ds(own, size), :].astype(bf16)
            theirs[z, which] = scr[which, pl.ds(other, size), :].astype(bf16)


def lift_kernel(pre_grad, cot, w_in, send, tall):
    j = pl.program_id(0)
    whole = cot[...].astype(f32).T + nt(w_in[...], pre_grad[...])
    for a in range(LONS // 4):
        tiles = [whole[q * 32 : (q + 1) * 32, a * 128 : (a + 1) * 128] for q in range(4)]
        for b, tile in enumerate(swap_quarters(tiles)):
            tall[pl.ds((4 * a + b) * GROUPS + j, PEERS, stride=SLAB), :] = tile

    @pl.when(j == pl.num_programs(0) - 1)
    def _():
        tall[TALL - 8 :, :] = jnp.zeros((8, 128), f32)
        to_slabs(tall, send)


def prep_kernel(place, row_w, cols, widths, chan, basis, own_mix, rim_mix, spread, token):
    token[...] = jnp.zeros(token.shape, f32)
    row_start, lon = place[0], place[1]
    high = lax.Precision.HIGHEST
    count = cols.shape[1]
    at = lax.broadcasted_iota(jnp.int32, (64, count), 0)
    rim = at % 4
    source = jnp.where(at < 32, at, jnp.where(at < 48, rim - REACH, rim + ROWS)) + row_start
    pick = (source == lax.broadcasted_iota(jnp.int32, (64, count), 1)).astype(f32)
    col = nt(pick, cols[...].astype(f32), high) - row_start.astype(f32)
    width = nt(pick, widths[...].astype(f32), high)
    lane = lax.broadcasted_iota(jnp.int32, (64, 128), 1)
    target = (lane % 32).astype(f32)
    hits = [
        jnp.where((col[:, s : s + 1] == target) & (width > s), 1.0, 0.0) for s in range(NB)
    ]
    chan_row = lax.broadcasted_iota(jnp.int32, (640, 640), 0)
    chan_lane = lax.broadcasted_iota(jnp.int32, (640, 640), 1)
    chan_pick = (chan_row == (chan_lane // 32) * 32 + lon).astype(f32)
    chan_w = nn(chan[...], chan_pick, high)
    rim_mix[...] = jnp.zeros(rim_mix.shape, bf16)
    quarter = lane[:32] // 32
    rim_at = lax.broadcasted_iota(jnp.int32, (16, 128), 0) // 4
    rim_quarter = lane[:16] // 32
    for k in range(NB):
        coef = nt(pick, row_w[k], high)
        weight = None
        for s in range(NB):
            term = coef[:, s : s + 1] * hits[s]
            weight = term if weight is None else weight + term
        for j in range(GROUPS):
            scaled = weight * chan_w[k : k + 1, 128 * j : 128 * (j + 1)]
            for q in range(4):
                own_mix[j, k * 128 + q * 32 : k * 128 + (q + 1) * 32, :] = jnp.where(
                    quarter == q, scaled[:32], 0.0
                ).astype(bf16)
            for side in range(2):
                part = scaled[32 + 16 * side : 48 + 16 * side]
                start = (k * 2 + side) * 128 + 16 * j
                rim_mix[start : start + 16, 128 * j : 128 * (j + 1)] = jnp.where(
                    rim_quarter == rim_at, part, 0.0
                ).astype(bf16)
        spread[k] = jnp.broadcast_to(basis[k : k + 1, :], (128, NLON)).T


def open_kernel(slabs, pick, _ready, moved, first, last, tall):
    from_slabs(slabs, tall)
    for j in range(GROUPS):
        moved[:, 128 * j : 128 * (j + 1)] = tall[pl.ds(j, NLON, stride=GROUPS), :].astype(bf16)
    edges = nn(moved[...], pick[...]).astype(bf16)
    last[...] = edges[:, :128]
    first[...] = edges[:, 128:]


def own_kernel(moved, forward, spread, own_mix, filtered, mixed):
    spectra = nn(forward[...], moved[...])
    first, second = spectra[:NF], spectra[NF:]
    for k in range(NB):
        cosine, sine = spread[k, :NF], spread[k, NF:]
        mixed[:NF, k * 128 : (k + 1) * 128] = (cosine * first + sine * second).astype(bf16)
        mixed[NF:, k * 128 : (k + 1) * 128] = (cosine * second - sine * first).astype(bf16)
    filtered[...] = nn(mixed[...], own_mix[0])


def close_kernel(filtered, before, after, forward, inverse, spread, rim_mix, send, mixed, tall):
    for side, rim in enumerate((before, after)):
        spectra = nn(forward[...], rim[...])
        first, second = spectra[:NF], spectra[NF:]
        for k in range(NB):
            cosine, sine = spread[k, :NF], spread[k, NF:]
            at = (k * 2 + side) * 128
            mixed[:NF, at : at + 128] = (cosine * first + sine * second).astype(bf16)
            mixed[NF:, at : at + 128] = (cosine * second - sine * first).astype(bf16)
    whole = (filtered[...] + nn(mixed[...], rim_mix[...])).astype(bf16)
    tall[TALL - 8 :, :] = jnp.zeros((8, 128), f32)
    for j in range(GROUPS):
        tall[pl.ds(j, NLON, stride=GROUPS), :] = nn(inverse[...], whole[:, 128 * j : 128 * (j + 1)])
    to_slabs(tall, send)


def merge_kernel(answer, column, out, piece, sem):
    rows = column[0, 0].astype(f32), column[0, 1].astype(f32)
    filled = 2 * rows[0].shape[0]
    fill = jnp.zeros((-filled % 128, rows[0].shape[1]), f32)
    turned = jnp.concatenate([rows[0], rows[1], fill], 0).T
    lane = lax.broadcasted_iota(jnp.int32, (8, 128), 1)
    for d in range(PEERS):
        own = turned[40 * d : 40 * (d + 1)]
        if filled == 80:
            end = own[32:]
            piece[d] = jnp.concatenate(
                [
                    own[:8] + pltpu.roll(jnp.where(lane < 48, end, 0.0), 80, 1),
                    own[8:16] + pltpu.roll(jnp.where(lane < 48, 0.0, end), 32, 1),
                    own[16:32],
                ],
                0,
            ).astype(bf16)
        else:
            for i in range(turned.shape[1] // 128):
                piece[d, 40 * i : 40 * (i + 1)] = own[:, 128 * i : 128 * (i + 1)].astype(bf16)
    copy = pltpu.make_async_copy(piece, out.at[:, PAD : PAD + piece.shape[1]], sem)
    copy.start()
    copy.wait()


def final_kernel(slabs, cot, out, grad_in, grad_out, tall):
    for d in range(PEERS):
        tall[SLAB * d : SLAB * d + PAD, :] = slabs[d, :PAD].astype(f32)
    for j in range(GROUPS):
        for a in range(LONS // 4):
            tiles = [tall[pl.ds((4 * a + b) * GROUPS + j, PEERS, stride=SLAB), :] for b in range(4)]
            turned = jnp.concatenate(tiles, 0).T
            for b, tile in enumerate(swap_quarters([turned[32 * q : 32 * (q + 1)] for q in range(4)])):
                rows = slice((4 * a + b) * 32, (4 * a + b + 1) * 32)
                lanes = slice(128 * j, 128 * (j + 1))
                out[rows, lanes] = (cot[rows, lanes].astype(f32) + tile).astype(bf16)
    size = grad_in.shape[0]
    total = slabs[0, PAD:].astype(f32)
    for d in range(1, PEERS):
        total = total + slabs[d, PAD:].astype(f32)
    if total.shape[0] == 32:
        lane = lax.broadcasted_iota(jnp.int32, (8, 128), 1)
        end = jnp.where(lane < 48, pltpu.roll(total[:8], 48, 1), pltpu.roll(total[8:16], 96, 1))
        total = jnp.concatenate([total, end], 0)
    elif total.shape[0] > 40:
        total = jnp.concatenate([total[i : i + 40] for i in range(0, total.shape[0], 40)], 1)
    lanes = total.shape[1]
    filled = jnp.concatenate([total, jnp.zeros((128 - 40, lanes), f32)], 0)
    grad_in[...] = filled.T[:size, :40]
    grad_out[...] = total[:, size : 2 * size]


def tables():
    lon = np.arange(NLON)
    freq = np.arange(NLON) % NF
    phase = (lon[:, None] * freq[None, :] % NLON) * (2.0 * math.pi / NLON)
    forward = np.where(np.arange(NLON)[None, :] >= NF, np.sin(phase), np.cos(phase))
    inverse = forward.T * (np.where(freq == 0, 1.0, 2.0) / NLON)[:, None]
    return jnp.asarray(forward.T, bf16), jnp.asarray(inverse.T, bf16)


def rim_picks():
    pick = np.zeros((640, 256), np.float32)
    for c in range(LOCAL):
        for r in range(REACH):
            pick[c * 32 + ROWS - REACH + r, c * 4 + r] = 1.0
            pick[c * 32 + r, 128 + c * 4 + r] = 1.0
    return jnp.asarray(pick, bf16)


def shape(*dims, dtype=bf16):
    return jax.ShapeDtypeStruct(dims, dtype)


VMEM = pl.BlockSpec(memory_space=pltpu.VMEM)
TOKEN = shape(8, 128, dtype=f32)
ANY = pl.BlockSpec(memory_space=pl.ANY)
SMEM = pl.BlockSpec(memory_space=pltpu.SMEM)


def call(kernel, out, ins, flops, moved, scratch=(), limit=24, **grid):
    options = dict(grid)
    if "grid" not in options:
        options["in_specs"] = ins
        options.setdefault("out_specs", jax.tree.map(lambda _: VMEM, out))
    return pl.pallas_call(
        kernel,
        out_shape=out,
        scratch_shapes=list(scratch),
        compiler_params=pltpu.CompilerParams(vmem_limit_bytes=limit << 20),
        cost_estimate=pl.CostEstimate(flops=int(flops), bytes_accessed=int(moved), transcendentals=0),
        **options,
    )


def body(mlp_input, out_cot, w_in, w_out, chan_weights, row_weights, basis_spectra, band_cols, band_widths):
    tokens_n = ROWS * LONS
    depth = lax.axis_size("z")
    n_lat = depth * lax.axis_size("core")
    part = 640 // n_lat
    lat, lon, core = lax.axis_index(LAT), lax.axis_index(LON), lax.axis_index("core")
    tokens = mlp_input.transpose(1, 0, 2).reshape(tokens_n, 640)
    cotangent = out_cot.transpose(1, 0, 2).reshape(tokens_n, 640)
    whole = lambda *dims: pl.BlockSpec(dims, lambda i: (0,) * len(dims))

    half = shape(depth, 2, part, 1280)
    half_spec = pl.BlockSpec((depth, 2, part, 640), lambda i: (0, 0, 0, i))
    pre_grad, mine, theirs = call(
        head_kernel,
        (pltpu.VMEM((tokens_n, 1280), bf16), pltpu.VMEM(half.shape, bf16), pltpu.VMEM(half.shape, bf16)),
        None,
        3e9,
        8e6,
        [pltpu.VMEM((640, tokens_n), bf16), pltpu.VMEM((640, tokens_n), bf16), pltpu.VMEM((2, 640, 640), f32)],
        limit=56,
        grid=(2,),
        in_specs=[
            SMEM,
            whole(tokens_n, 640),
            whole(tokens_n, 640),
            pl.BlockSpec((640, 640), lambda i: (0, i)),
            pl.BlockSpec((640, 640), lambda i: (i, 0)),
        ],
        out_specs=[pl.BlockSpec((tokens_n, 640), lambda i: (0, i)), half_spec, half_spec],
    )(core.reshape(1), tokens, cotangent, w_in, w_out)
    partner = lax.ppermute(theirs, "core", [(0, 1), (1, 0)])

    send = call(
        lift_kernel,
        shape(PEERS, PAD, 128),
        None,
        2e9,
        4e6,
        [pltpu.VMEM((TALL, 128), f32)],
        limit=48,
        grid=(GROUPS,),
        in_specs=[
            whole(tokens_n, 1280),
            pl.BlockSpec((tokens_n, 128), lambda j: (0, j)),
            pl.BlockSpec((128, 1280), lambda j: (j, 0)),
        ],
        out_specs=whole(PEERS, PAD, 128),
    )(pre_grad, cotangent, w_in)
    received = lax.all_to_all(send, LON, split_axis=0, concat_axis=0, tiled=True)

    mine, send = lax.optimization_barrier((mine, send))
    chip = (mine.astype(f32) + partner.astype(f32)).astype(bf16)
    column = lax.psum_scatter(chip, "z", scatter_dimension=0, tiled=True)

    own_mix, rim_mix, spread, ready = call(
        prep_kernel,
        (shape(GROUPS, NB * 128, 128), shape(NB * 256, 640), shape(NB, NLON, 128, dtype=f32), TOKEN),
        [SMEM] + [VMEM] * 5,
        1e9,
        6e6,
    )(
        jnp.stack([lat * ROWS, lon]).astype(jnp.int32),
        row_weights.transpose(0, 2, 1),
        band_cols.T,
        band_widths.reshape(1, -1),
        chan_weights,
        basis_spectra,
    )

    forward, inverse = tables()
    moved, first, last = call(
        open_kernel,
        (shape(NLON, 640), shape(NLON, 128), shape(NLON, 128)),
        [VMEM] * 3,
        1e8,
        2e6,
        [pltpu.VMEM((TALL, 128), f32)],
    )(received, rim_picks(), ready)
    up = [(i, i + 1) for i in range(n_lat - 1)]
    before = lax.ppermute(last, LAT, up)
    after = lax.ppermute(first, LAT, [(b, a) for a, b in up])

    filtered = call(
        own_kernel,
        shape(NLON, 640, dtype=f32),
        None,
        8e8,
        5e6,
        [pltpu.VMEM((NLON, NB * 128), bf16)],
        grid=(GROUPS,),
        in_specs=[
            pl.BlockSpec((NLON, 128), lambda j: (0, j)),
            whole(NLON, NLON),
            whole(NB, NLON, 128),
            pl.BlockSpec((1, NB * 128, 128), lambda j: (j, 0, 0)),
        ],
        out_specs=pl.BlockSpec((NLON, 128), lambda j: (0, j)),
    )(moved, forward, spread, own_mix)

    extra = 32 if part == 40 else 40 * -(-2 * part // 128)
    answer = call(
        close_kernel,
        shape(PEERS, PAD + extra, 128),
        None,
        1.5e9,
        7e6,
        [pltpu.VMEM((NLON, NB * 256), bf16), pltpu.VMEM((TALL, 128), f32)],
        grid=(1,),
        in_specs=[VMEM] * 7,
        out_specs=whole(PEERS, PAD, 128),
    )(filtered, before, after, forward, inverse, spread, rim_mix)
    merged = call(
        merge_kernel,
        shape(PEERS, PAD + extra, 128),
        [ANY, VMEM],
        1e6,
        2e6,
        [pltpu.VMEM((PEERS, extra, 128), bf16), pltpu.SemaphoreType.DMA],
        out_specs=ANY,
        input_output_aliases={0: 0},
    )(answer, column)
    returned = lax.all_to_all(merged, LON, split_axis=0, concat_axis=0, tiled=True)
    grid_grad, grad_in, grad_out = call(
        final_kernel,
        (shape(tokens_n, 640), shape(part, 40, dtype=f32), shape(40, part, dtype=f32)),
        [VMEM] * 2,
        1e8,
        2e6,
        [pltpu.VMEM((TALL, 128), f32)],
    )(returned, cotangent)
    grid_grad = grid_grad.reshape(LONS, ROWS, 640).transpose(1, 0, 2)
    return grid_grad, grad_in, grad_out


def solution(mesh):
    chips = Mesh(mesh.devices.reshape(-1, 2, 8, 4), ("z", "core", "y", "x"))
    grid = P(LAT, LON, None)
    return jax.shard_map(
        body,
        mesh=chips,
        in_specs=(grid, grid, P(), P(), P(), P(), P(), P(), P()),
        out_specs=(grid, P(LAT, LON), P(LON, LAT)),
        check_vma=False,
    )
```

```python
import functools
import math

import jax
import jax.numpy as jnp
import numpy as np
from jax import lax
from jax.experimental import pallas as pl
from jax.experimental.pallas import tpu as pltpu
from jax.sharding import Mesh, PartitionSpec as P

f32 = jnp.float32
bf16 = jnp.bfloat16
LAT = ("z", "core")
LON = ("y", "x")
ROWS = 32
LONS = 12
PEERS = 32
LOCAL = 20
NLON = 384
NF = 192
NB = 9
REACH = 4
GROUPS = 5
SLAB = LONS * GROUPS
PAD = 64
TALL = PEERS * SLAB + 8


def nt(a, b, precision=None):
    return lax.dot_general(a, b, (((1,), (1,)), ((), ())), preferred_element_type=f32, precision=precision)


def tn(a, b):
    return lax.dot_general(a, b, (((0,), (0,)), ((), ())), preferred_element_type=f32)


def nn(a, b, precision=None):
    return lax.dot_general(a, b, (((1,), (0,)), ((), ())), preferred_element_type=f32, precision=precision)


def swap_quarters(tiles):
    quarter = lax.broadcasted_iota(jnp.int32, tiles[0].shape, 1) // 32
    out = []
    for b in range(4):
        made = None
        for q in range(4):
            shift = (32 * (q - b)) % 128
            moved = pltpu.roll(tiles[q], shift, 1) if shift else tiles[q]
            made = moved if made is None else jnp.where(quarter == q, moved, made)
        out.append(made)
    return out


def gelu_parts(v):
    square = v * v
    tangent = jnp.tanh(0.7978845608 * (v + 0.044715 * v * square))
    half = 0.5 * (1.0 + tangent)
    slope = half + 0.5 * v * (1.0 - tangent * tangent) * 0.7978845608 * (1.0 + 0.134145 * square)
    return v * half, slope


def to_slabs(tall, out):
    for d in range(PEERS):
        out[d] = tall[SLAB * d : SLAB * d + PAD, :].astype(bf16)


def from_slabs(slabs, tall):
    for d in range(PEERS):
        tall[SLAB * d : SLAB * d + PAD, :] = slabs[d].astype(f32)


def head_kernel(core, tok, cot, w_in, w_out, pre_grad, mine, theirs, tok_t, cot_t, scr):
    @pl.when(pl.program_id(0) == 0)
    def _():
        tok_t[...] = tok[...].astype(f32).T.astype(bf16)
        cot_t[...] = cot[...].astype(f32).T.astype(bf16)

    gelu_value, slope = gelu_parts(nn(tok[...], w_in[...]))
    grad = (nt(cot[...], w_out[...]) * slope).astype(bf16)
    pre_grad[...] = grad
    c = core[0]
    depth, _, size = mine.shape[0], mine.shape[1], mine.shape[2]
    for which, (left, right) in enumerate(((tok_t, grad), (cot_t, gelu_value.astype(bf16)))):
        scr[which] = nn(left[...], right)
        for z in range(depth):
            own = pl.multiple_of((2 * z + c) * size, 8)
            other = pl.multiple_of((2 * z + 1 - c) * size, 8)
            mine[z, which] = scr[which, pl.ds(own, size), :].astype(bf16)
            theirs[z, which] = scr[which, pl.ds(other, size), :].astype(bf16)


def lift_kernel(pre_grad, cot, w_in, send, tall):
    j = pl.program_id(0)
    whole = cot[...].astype(f32).T + nt(w_in[...], pre_grad[...])
    for a in range(LONS // 4):
        tiles = [whole[q * 32 : (q + 1) * 32, a * 128 : (a + 1) * 128] for q in range(4)]
        for b, tile in enumerate(swap_quarters(tiles)):
            tall[pl.ds((4 * a + b) * GROUPS + j, PEERS, stride=SLAB), :] = tile

    @pl.when(j == pl.num_programs(0) - 1)
    def _():
        tall[TALL - 8 :, :] = jnp.zeros((8, 128), f32)
        to_slabs(tall, send)


def prep_kernel(place, row_w, cols, widths, chan, basis, own_mix, rim_mix, spread, token):
    token[...] = jnp.zeros(token.shape, f32)
    row_start, lon = place[0], place[1]
    high = lax.Precision.HIGHEST
    count = cols.shape[1]
    at = lax.broadcasted_iota(jnp.int32, (64, count), 0)
    rim = at % 4
    source = jnp.where(at < 32, at, jnp.where(at < 48, rim - REACH, rim + ROWS)) + row_start
    pick = (source == lax.broadcasted_iota(jnp.int32, (64, count), 1)).astype(f32)
    col = nt(pick, cols[...].astype(f32), high) - row_start.astype(f32)
    width = nt(pick, widths[...].astype(f32), high)
    lane = lax.broadcasted_iota(jnp.int32, (64, 128), 1)
    target = (lane % 32).astype(f32)
    hits = [
        jnp.where((col[:, s : s + 1] == target) & (width > s), 1.0, 0.0) for s in range(NB)
    ]
    chan_row = lax.broadcasted_iota(jnp.int32, (640, 640), 0)
    chan_lane = lax.broadcasted_iota(jnp.int32, (640, 640), 1)
    chan_pick = (chan_row == (chan_lane // 32) * 32 + lon).astype(f32)
    chan_w = nn(chan[...], chan_pick, high)
    rim_mix[...] = jnp.zeros(rim_mix.shape, bf16)
    quarter = lane[:32] // 32
    rim_at = lax.broadcasted_iota(jnp.int32, (16, 128), 0) // 4
    rim_quarter = lane[:16] // 32
    for k in range(NB):
        coef = nt(pick, row_w[k], high)
        weight = None
        for s in range(NB):
            term = coef[:, s : s + 1] * hits[s]
            weight = term if weight is None else weight + term
        for j in range(GROUPS):
            scaled = weight * chan_w[k : k + 1, 128 * j : 128 * (j + 1)]
            for q in range(4):
                own_mix[j, k * 128 + q * 32 : k * 128 + (q + 1) * 32, :] = jnp.where(
                    quarter == q, scaled[:32], 0.0
                ).astype(bf16)
            for side in range(2):
                part = scaled[32 + 16 * side : 48 + 16 * side]
                start = (k * 2 + side) * 128 + 16 * j
                rim_mix[start : start + 16, 128 * j : 128 * (j + 1)] = jnp.where(
                    rim_quarter == rim_at, part, 0.0
                ).astype(bf16)
        spread[k] = jnp.broadcast_to(basis[k : k + 1, :], (128, NLON)).T


def open_kernel(slabs, _ready, moved, first, last, tall):
    from_slabs(slabs, tall)
    for j in range(GROUPS):
        moved[:, 128 * j : 128 * (j + 1)] = tall[pl.ds(j, NLON, stride=GROUPS), :].astype(bf16)
    row = lax.broadcasted_iota(jnp.int32, (640, 256), 0)
    lane = lax.broadcasted_iota(jnp.int32, (640, 256), 1)
    edge = row % 32 - (ROWS - REACH) * (1 - lane // 128)
    pick = jnp.where(
        (lane % 128 - row // 32 * REACH == edge) & (edge >= 0) & (edge < REACH), 1.0, 0.0
    )
    edges = nn(moved[...], pick.astype(bf16)).astype(bf16)
    last[...] = edges[:, :128]
    first[...] = edges[:, 128:]


def own_kernel(moved, forward, spread, own_mix, filtered, mixed):
    spectra = nn(forward[...], moved[...])
    first, second = spectra[:NF], spectra[NF:]
    for k in range(NB):
        cosine, sine = spread[k, :NF], spread[k, NF:]
        mixed[:NF, k * 128 : (k + 1) * 128] = (cosine * first + sine * second).astype(bf16)
        mixed[NF:, k * 128 : (k + 1) * 128] = (cosine * second - sine * first).astype(bf16)
    filtered[...] = nn(mixed[...], own_mix[0])


def close_kernel(filtered, before, after, forward, inverse, spread, rim_mix, send, mixed, tall):
    for side, rim in enumerate((before, after)):
        spectra = nn(forward[...], rim[...])
        first, second = spectra[:NF], spectra[NF:]
        for k in range(NB):
            cosine, sine = spread[k, :NF], spread[k, NF:]
            at = (k * 2 + side) * 128
            mixed[:NF, at : at + 128] = (cosine * first + sine * second).astype(bf16)
            mixed[NF:, at : at + 128] = (cosine * second - sine * first).astype(bf16)
    whole = (filtered[...] + nn(mixed[...], rim_mix[...])).astype(bf16)
    tall[TALL - 8 :, :] = jnp.zeros((8, 128), f32)
    for j in range(GROUPS):
        tall[pl.ds(j, NLON, stride=GROUPS), :] = nn(inverse[...], whole[:, 128 * j : 128 * (j + 1)])
    to_slabs(tall, send)


def merge_kernel(answer, column, out, piece, sem):
    rows = column[0, 0].astype(f32), column[0, 1].astype(f32)
    filled = 2 * rows[0].shape[0]
    fill = jnp.zeros((-filled % 128, rows[0].shape[1]), f32)
    turned = jnp.concatenate([rows[0], rows[1], fill], 0).T
    lane = lax.broadcasted_iota(jnp.int32, (8, 128), 1)
    for d in range(PEERS):
        own = turned[40 * d : 40 * (d + 1)]
        if filled == 80:
            end = own[32:]
            piece[d] = jnp.concatenate(
                [
                    own[:8] + pltpu.roll(jnp.where(lane < 48, end, 0.0), 80, 1),
                    own[8:16] + pltpu.roll(jnp.where(lane < 48, 0.0, end), 32, 1),
                    own[16:32],
                ],
                0,
            ).astype(bf16)
        else:
            for i in range(turned.shape[1] // 128):
                piece[d, 40 * i : 40 * (i + 1)] = own[:, 128 * i : 128 * (i + 1)].astype(bf16)
    copy = pltpu.make_async_copy(piece, out.at[:, PAD : PAD + piece.shape[1]], sem)
    copy.start()
    copy.wait()


def final_kernel(slabs, cot, out, grad_in, grad_out, tall):
    for d in range(PEERS):
        tall[SLAB * d : SLAB * d + PAD, :] = slabs[d, :PAD].astype(f32)
    for j in range(GROUPS):
        for a in range(LONS // 4):
            tiles = [tall[pl.ds((4 * a + b) * GROUPS + j, PEERS, stride=SLAB), :] for b in range(4)]
            turned = jnp.concatenate(tiles, 0).T
            for b, tile in enumerate(swap_quarters([turned[32 * q : 32 * (q + 1)] for q in range(4)])):
                rows = slice((4 * a + b) * 32, (4 * a + b + 1) * 32)
                lanes = slice(128 * j, 128 * (j + 1))
                out[rows, lanes] = (cot[rows, lanes].astype(f32) + tile).astype(bf16)
    size = grad_in.shape[0]
    total = slabs[0, PAD:].astype(f32)
    for d in range(1, PEERS):
        total = total + slabs[d, PAD:].astype(f32)
    if total.shape[0] == 32:
        lane = lax.broadcasted_iota(jnp.int32, (8, 128), 1)
        end = jnp.where(lane < 48, pltpu.roll(total[:8], 48, 1), pltpu.roll(total[8:16], 96, 1))
        total = jnp.concatenate([total, end], 0)
    elif total.shape[0] > 40:
        total = jnp.concatenate([total[i : i + 40] for i in range(0, total.shape[0], 40)], 1)
    lanes = total.shape[1]
    filled = jnp.concatenate([total, jnp.zeros((128 - 40, lanes), f32)], 0)
    grad_in[...] = filled.T[:size, :40]
    grad_out[...] = total[:, size : 2 * size]


def tables():
    lon = np.arange(NLON)
    freq = np.arange(NLON) % NF
    phase = (lon[:, None] * freq[None, :] % NLON) * (2.0 * math.pi / NLON)
    forward = np.where(np.arange(NLON)[None, :] >= NF, np.sin(phase), np.cos(phase))
    inverse = forward.T * (np.where(freq == 0, 1.0, 2.0) / NLON)[:, None]
    return jnp.asarray(forward.T, bf16), jnp.asarray(inverse.T, bf16)


def shape(*dims, dtype=bf16):
    return jax.ShapeDtypeStruct(dims, dtype)


VMEM = pl.BlockSpec(memory_space=pltpu.VMEM)
TOKEN = shape(8, 128, dtype=f32)
ANY = pl.BlockSpec(memory_space=pl.ANY)
SMEM = pl.BlockSpec(memory_space=pltpu.SMEM)


def call(kernel, out, ins, flops, moved, scratch=(), limit=24, **grid):
    options = dict(grid)
    if "grid" not in options:
        options["in_specs"] = ins
        options.setdefault("out_specs", jax.tree.map(lambda _: VMEM, out))
    return pl.pallas_call(
        kernel,
        out_shape=out,
        scratch_shapes=list(scratch),
        compiler_params=pltpu.CompilerParams(vmem_limit_bytes=limit << 20),
        cost_estimate=pl.CostEstimate(flops=int(flops), bytes_accessed=int(moved), transcendentals=0),
        **options,
    )


def body(mlp_input, out_cot, w_in, w_out, chan_weights, row_weights, basis_spectra, band_cols, band_widths):
    tokens_n = ROWS * LONS
    depth = lax.axis_size("z")
    n_lat = depth * lax.axis_size("core")
    part = 640 // n_lat
    lat, lon, core = lax.axis_index(LAT), lax.axis_index(LON), lax.axis_index("core")
    tokens = mlp_input.transpose(1, 0, 2).reshape(tokens_n, 640)
    cotangent = out_cot.transpose(1, 0, 2).reshape(tokens_n, 640)
    whole = lambda *dims: pl.BlockSpec(dims, lambda i: (0,) * len(dims))

    half = shape(depth, 2, part, 1280)
    half_spec = pl.BlockSpec((depth, 2, part, 640), lambda i: (0, 0, 0, i))
    pre_grad, mine, theirs = call(
        head_kernel,
        (pltpu.VMEM((tokens_n, 1280), bf16), pltpu.VMEM(half.shape, bf16), pltpu.VMEM(half.shape, bf16)),
        None,
        3e9,
        8e6,
        [pltpu.VMEM((640, tokens_n), bf16), pltpu.VMEM((640, tokens_n), bf16), pltpu.VMEM((2, 640, 640), f32)],
        limit=56,
        grid=(2,),
        in_specs=[
            SMEM,
            whole(tokens_n, 640),
            whole(tokens_n, 640),
            pl.BlockSpec((640, 640), lambda i: (0, i)),
            pl.BlockSpec((640, 640), lambda i: (i, 0)),
        ],
        out_specs=[pl.BlockSpec((tokens_n, 640), lambda i: (0, i)), half_spec, half_spec],
    )(core.reshape(1), tokens, cotangent, w_in, w_out)
    partner = lax.ppermute(theirs, "core", [(0, 1), (1, 0)])

    send = call(
        lift_kernel,
        shape(PEERS, PAD, 128),
        None,
        2e9,
        4e6,
        [pltpu.VMEM((TALL, 128), f32)],
        limit=48,
        grid=(GROUPS,),
        in_specs=[
            whole(tokens_n, 1280),
            pl.BlockSpec((tokens_n, 128), lambda j: (0, j)),
            pl.BlockSpec((128, 1280), lambda j: (j, 0)),
        ],
        out_specs=whole(PEERS, PAD, 128),
    )(pre_grad, cotangent, w_in)
    received = lax.all_to_all(send, LON, split_axis=0, concat_axis=0, tiled=True)

    mine, send = lax.optimization_barrier((mine, send))
    chip = (mine.astype(f32) + partner.astype(f32)).astype(bf16)
    column = lax.psum_scatter(chip, "z", scatter_dimension=0, tiled=True)

    own_mix, rim_mix, spread, ready = call(
        prep_kernel,
        (pltpu.HBM((GROUPS, NB * 128, 128), bf16), shape(NB * 256, 640), shape(NB, NLON, 128, dtype=f32), TOKEN),
        [SMEM] + [VMEM] * 5,
        1e9,
        6e6,
    )(
        jnp.stack([lat * ROWS, lon]).astype(jnp.int32),
        row_weights.transpose(0, 2, 1),
        band_cols.T,
        band_widths.reshape(1, -1),
        chan_weights,
        basis_spectra,
    )

    forward, inverse = tables()
    moved, first, last = call(
        open_kernel,
        (shape(NLON, 640), shape(NLON, 128), shape(NLON, 128)),
        [VMEM] * 2,
        1e8,
        2e6,
        [pltpu.VMEM((TALL, 128), f32)],
    )(received, ready)
    up = [(i, i + 1) for i in range(n_lat - 1)]
    before = lax.ppermute(last, LAT, up)
    after = lax.ppermute(first, LAT, [(b, a) for a, b in up])

    filtered = call(
        own_kernel,
        shape(NLON, 640, dtype=f32),
        None,
        8e8,
        5e6,
        [pltpu.VMEM((NLON, NB * 128), bf16)],
        grid=(GROUPS,),
        in_specs=[
            pl.BlockSpec((NLON, 128), lambda j: (0, j)),
            whole(NLON, NLON),
            whole(NB, NLON, 128),
            pl.BlockSpec((1, NB * 128, 128), lambda j: (j, 0, 0)),
        ],
        out_specs=pl.BlockSpec((NLON, 128), lambda j: (0, j)),
    )(moved, forward, spread, pltpu.with_memory_space_constraint(own_mix, pltpu.HBM))

    extra = 32 if part == 40 else 40 * -(-2 * part // 128)
    answer = call(
        close_kernel,
        shape(PEERS, PAD + extra, 128),
        None,
        1.5e9,
        7e6,
        [pltpu.VMEM((NLON, NB * 256), bf16), pltpu.VMEM((TALL, 128), f32)],
        grid=(1,),
        in_specs=[VMEM] * 7,
        out_specs=whole(PEERS, PAD, 128),
    )(filtered, before, after, forward, inverse, spread, rim_mix)
    merged = call(
        merge_kernel,
        shape(PEERS, PAD + extra, 128),
        [ANY, VMEM],
        1e6,
        2e6,
        [pltpu.VMEM((PEERS, extra, 128), bf16), pltpu.SemaphoreType.DMA],
        out_specs=ANY,
        input_output_aliases={0: 0},
    )(answer, pltpu.with_memory_space_constraint(column, pltpu.HBM))
    returned = lax.all_to_all(merged, LON, split_axis=0, concat_axis=0, tiled=True)
    grid_grad, grad_in, grad_out = call(
        final_kernel,
        (shape(tokens_n, 640), shape(part, 40, dtype=f32), shape(40, part, dtype=f32)),
        [VMEM] * 2,
        1e8,
        2e6,
        [pltpu.VMEM((TALL, 128), f32)],
    )(returned, cotangent)
    grid_grad = grid_grad.reshape(LONS, ROWS, 640).transpose(1, 0, 2)
    return grid_grad, grad_in, grad_out


def solution(mesh):
    chips = Mesh(mesh.devices.reshape(-1, 2, 8, 4), ("z", "core", "y", "x"))
    grid = P(LAT, LON, None)
    return jax.shard_map(
        body,
        mesh=chips,
        in_specs=(grid, grid, P(), P(), P(), P(), P(), P(), P()),
        out_specs=(grid, P(LAT, LON), P(LON, LAT)),
        check_vma=False,
    )
```

```python
import functools
import math

import jax
import jax.numpy as jnp
import numpy as np
from jax import lax
from jax.experimental import pallas as pl
from jax.experimental.pallas import tpu as pltpu
from jax.sharding import Mesh, PartitionSpec as P

f32 = jnp.float32
bf16 = jnp.bfloat16
LAT = ("z", "core")
LON = ("y", "x")
ROWS = 32
LONS = 12
PEERS = 32
LOCAL = 20
NLON = 384
NF = 192
NB = 9
REACH = 4
GROUPS = 5
SLAB = LONS * GROUPS
PAD = 64
TALL = PEERS * SLAB + 8


def nt(a, b, precision=None):
    return lax.dot_general(a, b, (((1,), (1,)), ((), ())), preferred_element_type=f32, precision=precision)


def tn(a, b):
    return lax.dot_general(a, b, (((0,), (0,)), ((), ())), preferred_element_type=f32)


def nn(a, b, precision=None):
    return lax.dot_general(a, b, (((1,), (0,)), ((), ())), preferred_element_type=f32, precision=precision)


def swap_quarters(tiles):
    quarter = lax.broadcasted_iota(jnp.int32, tiles[0].shape, 1) // 32
    out = []
    for b in range(4):
        made = None
        for q in range(4):
            shift = (32 * (q - b)) % 128
            moved = pltpu.roll(tiles[q], shift, 1) if shift else tiles[q]
            made = moved if made is None else jnp.where(quarter == q, moved, made)
        out.append(made)
    return out


def gelu_parts(v):
    square = v * v
    tangent = jnp.tanh(0.7978845608 * (v + 0.044715 * v * square))
    half = 0.5 * (1.0 + tangent)
    slope = half + 0.5 * v * (1.0 - tangent * tangent) * 0.7978845608 * (1.0 + 0.134145 * square)
    return v * half, slope


def to_slabs(tall, out):
    for d in range(PEERS):
        out[d] = tall[SLAB * d : SLAB * d + PAD, :].astype(bf16)


def from_slabs(slabs, tall):
    for d in range(PEERS):
        tall[SLAB * d : SLAB * d + PAD, :] = slabs[d].astype(f32)


def head_kernel(core, tok, cot, w_in, w_out, pre_grad, mine, theirs, tok_t, cot_t, scr):
    @pl.when(pl.program_id(0) == 0)
    def _():
        tok_t[...] = tok[...].astype(f32).T.astype(bf16)
        cot_t[...] = cot[...].astype(f32).T.astype(bf16)

    gelu_value, slope = gelu_parts(nn(tok[...], w_in[...]))
    grad = (nt(cot[...], w_out[...]) * slope).astype(bf16)
    pre_grad[...] = grad
    c = core[0]
    depth, _, size = mine.shape[0], mine.shape[1], mine.shape[2]
    for which, (left, right) in enumerate(((tok_t, grad), (cot_t, gelu_value.astype(bf16)))):
        scr[which] = nn(left[...], right)
        for z in range(depth):
            own = pl.multiple_of((2 * z + c) * size, 8)
            other = pl.multiple_of((2 * z + 1 - c) * size, 8)
            mine[z, which] = scr[which, pl.ds(own, size), :].astype(bf16)
            theirs[z, which] = scr[which, pl.ds(other, size), :].astype(bf16)


def lift_kernel(pre_grad, cot, w_in, send, tall):
    tall[TALL - 8 :, :] = jnp.zeros((8, 128), f32)
    for j in range(GROUPS):
        part = slice(128 * j, 128 * (j + 1))
        whole = cot[:, part].astype(f32).T + nt(w_in[part, :], pre_grad[...])
        for a in range(LONS // 4):
            tiles = [whole[q * 32 : (q + 1) * 32, a * 128 : (a + 1) * 128] for q in range(4)]
            for b, tile in enumerate(swap_quarters(tiles)):
                tall[pl.ds((4 * a + b) * GROUPS + j, PEERS, stride=SLAB), :] = tile
    to_slabs(tall, send)


def prep_kernel(place, row_w, cols, widths, chan, basis, own_mix, rim_mix, spread, token):
    token[...] = jnp.zeros(token.shape, f32)
    row_start, lon = place[0], place[1]
    high = lax.Precision.HIGHEST
    count = cols.shape[1]
    at = lax.broadcasted_iota(jnp.int32, (64, count), 0)
    rim = at % 4
    source = jnp.where(at < 32, at, jnp.where(at < 48, rim - REACH, rim + ROWS)) + row_start
    pick = (source == lax.broadcasted_iota(jnp.int32, (64, count), 1)).astype(f32)
    col = nt(pick, cols[...].astype(f32), high) - row_start.astype(f32)
    width = nt(pick, widths[...].astype(f32), high)
    lane = lax.broadcasted_iota(jnp.int32, (64, 128), 1)
    target = (lane % 32).astype(f32)
    hits = [
        jnp.where((col[:, s : s + 1] == target) & (width > s), 1.0, 0.0) for s in range(NB)
    ]
    chan_row = lax.broadcasted_iota(jnp.int32, (640, 640), 0)
    chan_lane = lax.broadcasted_iota(jnp.int32, (640, 640), 1)
    chan_pick = (chan_row == (chan_lane // 32) * 32 + lon).astype(f32)
    chan_w = nn(chan[...], chan_pick, high)
    rim_mix[...] = jnp.zeros(rim_mix.shape, bf16)
    quarter = lane[:32] // 32
    rim_at = lax.broadcasted_iota(jnp.int32, (16, 128), 0) // 4
    rim_quarter = lane[:16] // 32
    for k in range(NB):
        coef = nt(pick, row_w[k], high)
        weight = None
        for s in range(NB):
            term = coef[:, s : s + 1] * hits[s]
            weight = term if weight is None else weight + term
        for j in range(GROUPS):
            scaled = weight * chan_w[k : k + 1, 128 * j : 128 * (j + 1)]
            for q in range(4):
                own_mix[j, k * 128 + q * 32 : k * 128 + (q + 1) * 32, :] = jnp.where(
                    quarter == q, scaled[:32], 0.0
                ).astype(bf16)
            for side in range(2):
                part = scaled[32 + 16 * side : 48 + 16 * side]
                start = (k * 2 + side) * 128 + 16 * j
                rim_mix[start : start + 16, 128 * j : 128 * (j + 1)] = jnp.where(
                    rim_quarter == rim_at, part, 0.0
                ).astype(bf16)
        spread[k] = jnp.broadcast_to(basis[k : k + 1, :], (128, NLON)).T


def open_kernel(slabs, _ready, moved, first, last, tall):
    from_slabs(slabs, tall)
    for j in range(GROUPS):
        moved[:, 128 * j : 128 * (j + 1)] = tall[pl.ds(j, NLON, stride=GROUPS), :].astype(bf16)
    row = lax.broadcasted_iota(jnp.int32, (640, 256), 0)
    lane = lax.broadcasted_iota(jnp.int32, (640, 256), 1)
    edge = row % 32 - (ROWS - REACH) * (1 - lane // 128)
    pick = jnp.where(
        (lane % 128 - row // 32 * REACH == edge) & (edge >= 0) & (edge < REACH), 1.0, 0.0
    )
    edges = nn(moved[...], pick.astype(bf16)).astype(bf16)
    last[...] = edges[:, :128]
    first[...] = edges[:, 128:]


def own_kernel(moved, forward, spread, own_mix, filtered, mixed):
    spectra = nn(forward[...], moved[...])
    first, second = spectra[:NF], spectra[NF:]
    for k in range(NB):
        cosine, sine = spread[k, :NF], spread[k, NF:]
        mixed[:NF, k * 128 : (k + 1) * 128] = (cosine * first + sine * second).astype(bf16)
        mixed[NF:, k * 128 : (k + 1) * 128] = (cosine * second - sine * first).astype(bf16)
    filtered[...] = nn(mixed[...], own_mix[0])


def close_kernel(filtered, before, after, forward, inverse, spread, rim_mix, send, mixed, tall):
    for side, rim in enumerate((before, after)):
        spectra = nn(forward[...], rim[...])
        first, second = spectra[:NF], spectra[NF:]
        for k in range(NB):
            cosine, sine = spread[k, :NF], spread[k, NF:]
            at = (k * 2 + side) * 128
            mixed[:NF, at : at + 128] = (cosine * first + sine * second).astype(bf16)
            mixed[NF:, at : at + 128] = (cosine * second - sine * first).astype(bf16)
    whole = (filtered[...] + nn(mixed[...], rim_mix[...])).astype(bf16)
    tall[TALL - 8 :, :] = jnp.zeros((8, 128), f32)
    for j in range(GROUPS):
        tall[pl.ds(j, NLON, stride=GROUPS), :] = nn(inverse[...], whole[:, 128 * j : 128 * (j + 1)])
    to_slabs(tall, send)


def merge_kernel(answer, column, out, piece, sem):
    rows = column[0, 0].astype(f32), column[0, 1].astype(f32)
    filled = 2 * rows[0].shape[0]
    fill = jnp.zeros((-filled % 128, rows[0].shape[1]), f32)
    turned = jnp.concatenate([rows[0], rows[1], fill], 0).T
    lane = lax.broadcasted_iota(jnp.int32, (8, 128), 1)
    for d in range(PEERS):
        own = turned[40 * d : 40 * (d + 1)]
        if filled == 80:
            end = own[32:]
            piece[d] = jnp.concatenate(
                [
                    own[:8] + pltpu.roll(jnp.where(lane < 48, end, 0.0), 80, 1),
                    own[8:16] + pltpu.roll(jnp.where(lane < 48, 0.0, end), 32, 1),
                    own[16:32],
                ],
                0,
            ).astype(bf16)
        else:
            for i in range(turned.shape[1] // 128):
                piece[d, 40 * i : 40 * (i + 1)] = own[:, 128 * i : 128 * (i + 1)].astype(bf16)
    copy = pltpu.make_async_copy(piece, out.at[:, PAD : PAD + piece.shape[1]], sem)
    copy.start()
    copy.wait()


def final_kernel(slabs, cot, out, grad_in, grad_out, tall):
    for d in range(PEERS):
        tall[SLAB * d : SLAB * d + PAD, :] = slabs[d, :PAD].astype(f32)
    for j in range(GROUPS):
        for a in range(LONS // 4):
            tiles = [tall[pl.ds((4 * a + b) * GROUPS + j, PEERS, stride=SLAB), :] for b in range(4)]
            turned = jnp.concatenate(tiles, 0).T
            for b, tile in enumerate(swap_quarters([turned[32 * q : 32 * (q + 1)] for q in range(4)])):
                rows = slice((4 * a + b) * 32, (4 * a + b + 1) * 32)
                lanes = slice(128 * j, 128 * (j + 1))
                out[rows, lanes] = (cot[rows, lanes].astype(f32) + tile).astype(bf16)
    size = grad_in.shape[0]
    total = slabs[0, PAD:].astype(f32)
    for d in range(1, PEERS):
        total = total + slabs[d, PAD:].astype(f32)
    if total.shape[0] == 32:
        lane = lax.broadcasted_iota(jnp.int32, (8, 128), 1)
        end = jnp.where(lane < 48, pltpu.roll(total[:8], 48, 1), pltpu.roll(total[8:16], 96, 1))
        total = jnp.concatenate([total, end], 0)
    elif total.shape[0] > 40:
        total = jnp.concatenate([total[i : i + 40] for i in range(0, total.shape[0], 40)], 1)
    lanes = total.shape[1]
    filled = jnp.concatenate([total, jnp.zeros((128 - 40, lanes), f32)], 0)
    grad_in[...] = filled.T[:size, :40]
    grad_out[...] = total[:, size : 2 * size]


def tables():
    lon = np.arange(NLON)
    freq = np.arange(NLON) % NF
    phase = (lon[:, None] * freq[None, :] % NLON) * (2.0 * math.pi / NLON)
    forward = np.where(np.arange(NLON)[None, :] >= NF, np.sin(phase), np.cos(phase))
    inverse = forward.T * (np.where(freq == 0, 1.0, 2.0) / NLON)[:, None]
    return jnp.asarray(forward.T, bf16), jnp.asarray(inverse.T, bf16)


def shape(*dims, dtype=bf16):
    return jax.ShapeDtypeStruct(dims, dtype)


VMEM = pl.BlockSpec(memory_space=pltpu.VMEM)
TOKEN = shape(8, 128, dtype=f32)
ANY = pl.BlockSpec(memory_space=pl.ANY)
SMEM = pl.BlockSpec(memory_space=pltpu.SMEM)


def call(kernel, out, ins, flops, moved, scratch=(), limit=24, **grid):
    options = dict(grid)
    if "grid" not in options:
        options["in_specs"] = ins
        options.setdefault("out_specs", jax.tree.map(lambda _: VMEM, out))
    return pl.pallas_call(
        kernel,
        out_shape=out,
        scratch_shapes=list(scratch),
        compiler_params=pltpu.CompilerParams(vmem_limit_bytes=limit << 20),
        cost_estimate=pl.CostEstimate(flops=int(flops), bytes_accessed=int(moved), transcendentals=0),
        **options,
    )


def body(mlp_input, out_cot, w_in, w_out, chan_weights, row_weights, basis_spectra, band_cols, band_widths):
    tokens_n = ROWS * LONS
    depth = lax.axis_size("z")
    n_lat = depth * lax.axis_size("core")
    part = 640 // n_lat
    lat, lon, core = lax.axis_index(LAT), lax.axis_index(LON), lax.axis_index("core")
    tokens = mlp_input.transpose(1, 0, 2).reshape(tokens_n, 640)
    cotangent = out_cot.transpose(1, 0, 2).reshape(tokens_n, 640)
    whole = lambda *dims: pl.BlockSpec(dims, lambda i: (0,) * len(dims))

    half = shape(depth, 2, part, 1280)
    half_spec = pl.BlockSpec((depth, 2, part, 640), lambda i: (0, 0, 0, i))
    pre_grad, mine, theirs = call(
        head_kernel,
        (pltpu.VMEM((tokens_n, 1280), bf16), pltpu.VMEM(half.shape, bf16), pltpu.VMEM(half.shape, bf16)),
        None,
        3e9,
        8e6,
        [pltpu.VMEM((640, tokens_n), bf16), pltpu.VMEM((640, tokens_n), bf16), pltpu.VMEM((2, 640, 640), f32)],
        limit=56,
        grid=(2,),
        in_specs=[
            SMEM,
            whole(tokens_n, 640),
            whole(tokens_n, 640),
            pl.BlockSpec((640, 640), lambda i: (0, i)),
            pl.BlockSpec((640, 640), lambda i: (i, 0)),
        ],
        out_specs=[pl.BlockSpec((tokens_n, 640), lambda i: (0, i)), half_spec, half_spec],
    )(core.reshape(1), tokens, cotangent, w_in, w_out)
    partner = lax.ppermute(theirs, "core", [(0, 1), (1, 0)])

    send = call(
        lift_kernel,
        pltpu.HBM((PEERS, PAD, 128), bf16),
        None,
        2e9,
        4e6,
        [pltpu.VMEM((TALL, 128), f32)],
        limit=48,
        grid=(1,),
        in_specs=[VMEM] * 3,
        out_specs=whole(PEERS, PAD, 128),
    )(pre_grad, cotangent, w_in)
    received = lax.all_to_all(send, LON, split_axis=0, concat_axis=0, tiled=True)

    mine, send = lax.optimization_barrier((mine, send))
    chip = (mine.astype(f32) + partner.astype(f32)).astype(bf16)
    column = lax.psum_scatter(chip, "z", scatter_dimension=0, tiled=True)

    own_mix, rim_mix, spread, ready = call(
        prep_kernel,
        (pltpu.HBM((GROUPS, NB * 128, 128), bf16), shape(NB * 256, 640), shape(NB, NLON, 128, dtype=f32), TOKEN),
        [SMEM] + [VMEM] * 5,
        1e9,
        6e6,
    )(
        jnp.stack([lat * ROWS, lon]).astype(jnp.int32),
        row_weights.transpose(0, 2, 1),
        band_cols.T,
        band_widths.reshape(1, -1),
        chan_weights,
        basis_spectra,
    )

    forward, inverse = tables()
    moved, first, last = call(
        open_kernel,
        (shape(NLON, 640), shape(NLON, 128), shape(NLON, 128)),
        [VMEM] * 2,
        1e8,
        2e6,
        [pltpu.VMEM((TALL, 128), f32)],
    )(received, ready)
    up = [(i, i + 1) for i in range(n_lat - 1)]
    before = lax.ppermute(last, LAT, up)
    after = lax.ppermute(first, LAT, [(b, a) for a, b in up])

    filtered = call(
        own_kernel,
        shape(NLON, 640, dtype=f32),
        None,
        8e8,
        5e6,
        [pltpu.VMEM((NLON, NB * 128), bf16)],
        grid=(GROUPS,),
        in_specs=[
            pl.BlockSpec((NLON, 128), lambda j: (0, j)),
            whole(NLON, NLON),
            whole(NB, NLON, 128),
            pl.BlockSpec((1, NB * 128, 128), lambda j: (j, 0, 0)),
        ],
        out_specs=pl.BlockSpec((NLON, 128), lambda j: (0, j)),
    )(moved, forward, spread, pltpu.with_memory_space_constraint(own_mix, pltpu.HBM))

    extra = 32 if part == 40 else 40 * -(-2 * part // 128)
    answer = call(
        close_kernel,
        shape(PEERS, PAD + extra, 128),
        None,
        1.5e9,
        7e6,
        [pltpu.VMEM((NLON, NB * 256), bf16), pltpu.VMEM((TALL, 128), f32)],
        grid=(1,),
        in_specs=[VMEM] * 7,
        out_specs=whole(PEERS, PAD, 128),
    )(filtered, before, after, forward, inverse, spread, rim_mix)
    merged = call(
        merge_kernel,
        shape(PEERS, PAD + extra, 128),
        [ANY, VMEM],
        1e6,
        2e6,
        [pltpu.VMEM((PEERS, extra, 128), bf16), pltpu.SemaphoreType.DMA],
        out_specs=ANY,
        input_output_aliases={0: 0},
    )(answer, pltpu.with_memory_space_constraint(column, pltpu.HBM))
    returned = lax.all_to_all(merged, LON, split_axis=0, concat_axis=0, tiled=True)
    grid_grad, grad_in, grad_out = call(
        final_kernel,
        (shape(tokens_n, 640), shape(part, 40, dtype=f32), shape(40, part, dtype=f32)),
        [VMEM] * 2,
        1e8,
        2e6,
        [pltpu.VMEM((TALL, 128), f32)],
    )(returned, cotangent)
    grid_grad = grid_grad.reshape(LONS, ROWS, 640).transpose(1, 0, 2)
    return grid_grad, grad_in, grad_out


def solution(mesh):
    chips = Mesh(mesh.devices.reshape(-1, 2, 8, 4), ("z", "core", "y", "x"))
    grid = P(LAT, LON, None)
    return jax.shard_map(
        body,
        mesh=chips,
        in_specs=(grid, grid, P(), P(), P(), P(), P(), P(), P()),
        out_specs=(grid, P(LAT, LON), P(LON, LAT)),
        check_vma=False,
    )
```

```python
import functools
import math

import jax
import jax.numpy as jnp
import numpy as np
from jax import lax
from jax.experimental import pallas as pl
from jax.experimental.pallas import tpu as pltpu
from jax.sharding import Mesh, PartitionSpec as P

f32 = jnp.float32
bf16 = jnp.bfloat16
LAT = ("z", "core")
LON = ("y", "x")
ROWS = 32
LONS = 12
PEERS = 32
LOCAL = 20
NLON = 384
NF = 192
NB = 9
REACH = 4
GROUPS = 5
SLAB = LONS * GROUPS
PAD = 64
TALL = PEERS * SLAB + 8


def nt(a, b, precision=None):
    return lax.dot_general(a, b, (((1,), (1,)), ((), ())), preferred_element_type=f32, precision=precision)


def tn(a, b):
    return lax.dot_general(a, b, (((0,), (0,)), ((), ())), preferred_element_type=f32)


def nn(a, b, precision=None):
    return lax.dot_general(a, b, (((1,), (0,)), ((), ())), preferred_element_type=f32, precision=precision)


def swap_quarters(tiles):
    quarter = lax.broadcasted_iota(jnp.int32, tiles[0].shape, 1) // 32
    out = []
    for b in range(4):
        made = None
        for q in range(4):
            shift = (32 * (q - b)) % 128
            moved = pltpu.roll(tiles[q], shift, 1) if shift else tiles[q]
            made = moved if made is None else jnp.where(quarter == q, moved, made)
        out.append(made)
    return out


def gelu_parts(v):
    square = v * v
    tangent = jnp.tanh(0.7978845608 * (v + 0.044715 * v * square))
    half = 0.5 * (1.0 + tangent)
    slope = half + 0.5 * v * (1.0 - tangent * tangent) * 0.7978845608 * (1.0 + 0.134145 * square)
    return v * half, slope


def to_slabs(tall, out):
    for d in range(PEERS):
        out[d] = tall[SLAB * d : SLAB * d + PAD, :].astype(bf16)


def from_slabs(slabs, tall):
    for d in range(PEERS):
        tall[SLAB * d : SLAB * d + PAD, :] = slabs[d].astype(f32)


def head_kernel(core, tok, cot, w_in, w_out, pre_grad, mine, theirs, tok_t, cot_t, scr):
    @pl.when(pl.program_id(0) == 0)
    def _():
        tok_t[...] = tok[...].astype(f32).T.astype(bf16)
        cot_t[...] = cot[...].astype(f32).T.astype(bf16)

    gelu_value, slope = gelu_parts(nn(tok[...], w_in[...]))
    grad = (nt(cot[...], w_out[...]) * slope).astype(bf16)
    pre_grad[...] = grad
    c = core[0]
    depth, _, size = mine.shape[0], mine.shape[1], mine.shape[2]
    for which, (left, right) in enumerate(((tok_t, grad), (cot_t, gelu_value.astype(bf16)))):
        scr[which] = nn(left[...], right)
        for z in range(depth):
            own = pl.multiple_of((2 * z + c) * size, 8)
            other = pl.multiple_of((2 * z + 1 - c) * size, 8)
            mine[z, which] = scr[which, pl.ds(own, size), :].astype(bf16)
            theirs[z, which] = scr[which, pl.ds(other, size), :].astype(bf16)


def lift_kernel(pre_grad, cot, w_in, send, tall):
    tall[TALL - 8 :, :] = jnp.zeros((8, 128), f32)
    for j in range(GROUPS):
        part = slice(128 * j, 128 * (j + 1))
        whole = cot[:, part].astype(f32).T + nt(w_in[part, :], pre_grad[...])
        for a in range(LONS // 4):
            tiles = [whole[q * 32 : (q + 1) * 32, a * 128 : (a + 1) * 128] for q in range(4)]
            for b, tile in enumerate(swap_quarters(tiles)):
                tall[pl.ds((4 * a + b) * GROUPS + j, PEERS, stride=SLAB), :] = tile
    to_slabs(tall, send)


def prep_kernel(place, row_w, cols, widths, chan, basis, own_mix, rim_mix, spread, token):
    token[...] = jnp.zeros(token.shape, f32)
    row_start, lon = place[0], place[1]
    high = lax.Precision.HIGHEST
    count = cols.shape[1]
    at = lax.broadcasted_iota(jnp.int32, (64, count), 0)
    rim = at % 4
    source = jnp.where(at < 32, at, jnp.where(at < 48, rim - REACH, rim + ROWS)) + row_start
    pick = (source == lax.broadcasted_iota(jnp.int32, (64, count), 1)).astype(f32)
    col = nt(pick, cols[...].astype(f32), high) - row_start.astype(f32)
    width = nt(pick, widths[...].astype(f32), high)
    lane = lax.broadcasted_iota(jnp.int32, (64, 128), 1)
    target = (lane % 32).astype(f32)
    hits = [
        jnp.where((col[:, s : s + 1] == target) & (width > s), 1.0, 0.0) for s in range(NB)
    ]
    chan_row = lax.broadcasted_iota(jnp.int32, (640, 640), 0)
    chan_lane = lax.broadcasted_iota(jnp.int32, (640, 640), 1)
    chan_pick = (chan_row == (chan_lane // 32) * 32 + lon).astype(f32)
    chan_w = nn(chan[...], chan_pick, high)
    rim_mix[...] = jnp.zeros(rim_mix.shape, bf16)
    quarter = lane[:32] // 32
    rim_at = lax.broadcasted_iota(jnp.int32, (16, 128), 0) // 4
    rim_quarter = lane[:16] // 32
    for k in range(NB):
        coef = nt(pick, row_w[k], high)
        weight = None
        for s in range(NB):
            term = coef[:, s : s + 1] * hits[s]
            weight = term if weight is None else weight + term
        for j in range(GROUPS):
            scaled = weight * chan_w[k : k + 1, 128 * j : 128 * (j + 1)]
            for q in range(4):
                own_mix[j, k * 128 + q * 32 : k * 128 + (q + 1) * 32, :] = jnp.where(
                    quarter == q, scaled[:32], 0.0
                ).astype(bf16)
            for side in range(2):
                part = scaled[32 + 16 * side : 48 + 16 * side]
                start = (k * 2 + side) * 128 + 16 * j
                rim_mix[start : start + 16, 128 * j : 128 * (j + 1)] = jnp.where(
                    rim_quarter == rim_at, part, 0.0
                ).astype(bf16)
        spread[k] = jnp.broadcast_to(basis[k : k + 1, :], (128, NLON)).T


def open_kernel(slabs, _ready, moved, first, last, tall):
    from_slabs(slabs, tall)
    for j in range(GROUPS):
        moved[:, 128 * j : 128 * (j + 1)] = tall[pl.ds(j, NLON, stride=GROUPS), :].astype(bf16)
    row = lax.broadcasted_iota(jnp.int32, (640, 256), 0)
    lane = lax.broadcasted_iota(jnp.int32, (640, 256), 1)
    edge = row % 32 - (ROWS - REACH) * (1 - lane // 128)
    pick = jnp.where(
        (lane % 128 - row // 32 * REACH == edge) & (edge >= 0) & (edge < REACH), 1.0, 0.0
    )
    edges = nn(moved[...], pick.astype(bf16)).astype(bf16)
    last[...] = edges[:, :128]
    first[...] = edges[:, 128:]


def own_kernel(moved, forward, spread, own_mix, filtered, mixed, held, sems):
    copies = [pltpu.make_async_copy(own_mix.at[j], held.at[j], sems.at[j]) for j in range(GROUPS)]
    for copy in copies:
        copy.start()
    for j in range(GROUPS):
        lanes = slice(128 * j, 128 * (j + 1))
        spectra = nn(forward[...], moved[:, lanes])
        first, second = spectra[:NF], spectra[NF:]
        for k in range(NB):
            cosine, sine = spread[k, :NF], spread[k, NF:]
            mixed[j % 2, :NF, k * 128 : (k + 1) * 128] = (cosine * first + sine * second).astype(bf16)
            mixed[j % 2, NF:, k * 128 : (k + 1) * 128] = (cosine * second - sine * first).astype(bf16)
        copies[j].wait()
        filtered[:, lanes] = nn(mixed[j % 2], held[j])


def close_kernel(filtered, before, after, forward, inverse, spread, rim_mix, send, mixed, tall):
    for side, rim in enumerate((before, after)):
        spectra = nn(forward[...], rim[...])
        first, second = spectra[:NF], spectra[NF:]
        for k in range(NB):
            cosine, sine = spread[k, :NF], spread[k, NF:]
            at = (k * 2 + side) * 128
            mixed[:NF, at : at + 128] = (cosine * first + sine * second).astype(bf16)
            mixed[NF:, at : at + 128] = (cosine * second - sine * first).astype(bf16)
    whole = (filtered[...] + nn(mixed[...], rim_mix[...])).astype(bf16)
    tall[TALL - 8 :, :] = jnp.zeros((8, 128), f32)
    for j in range(GROUPS):
        tall[pl.ds(j, NLON, stride=GROUPS), :] = nn(inverse[...], whole[:, 128 * j : 128 * (j + 1)])
    to_slabs(tall, send)


def merge_kernel(answer, column, out, piece, sem):
    rows = column[0, 0].astype(f32), column[0, 1].astype(f32)
    filled = 2 * rows[0].shape[0]
    fill = jnp.zeros((-filled % 128, rows[0].shape[1]), f32)
    turned = jnp.concatenate([rows[0], rows[1], fill], 0).T
    lane = lax.broadcasted_iota(jnp.int32, (8, 128), 1)
    for d in range(PEERS):
        own = turned[40 * d : 40 * (d + 1)]
        if filled == 80:
            end = own[32:]
            piece[d] = jnp.concatenate(
                [
                    own[:8] + pltpu.roll(jnp.where(lane < 48, end, 0.0), 80, 1),
                    own[8:16] + pltpu.roll(jnp.where(lane < 48, 0.0, end), 32, 1),
                    own[16:32],
                ],
                0,
            ).astype(bf16)
        else:
            for i in range(turned.shape[1] // 128):
                piece[d, 40 * i : 40 * (i + 1)] = own[:, 128 * i : 128 * (i + 1)].astype(bf16)
    copy = pltpu.make_async_copy(piece, out.at[:, PAD : PAD + piece.shape[1]], sem)
    copy.start()
    copy.wait()


def final_kernel(slabs, cot, out, grad_in, grad_out, tall):
    for d in range(PEERS):
        tall[SLAB * d : SLAB * d + PAD, :] = slabs[d, :PAD].astype(f32)
    for j in range(GROUPS):
        for a in range(LONS // 4):
            tiles = [tall[pl.ds((4 * a + b) * GROUPS + j, PEERS, stride=SLAB), :] for b in range(4)]
            turned = jnp.concatenate(tiles, 0).T
            for b, tile in enumerate(swap_quarters([turned[32 * q : 32 * (q + 1)] for q in range(4)])):
                rows = slice((4 * a + b) * 32, (4 * a + b + 1) * 32)
                lanes = slice(128 * j, 128 * (j + 1))
                out[rows, lanes] = (cot[rows, lanes].astype(f32) + tile).astype(bf16)
    size = grad_in.shape[0]
    total = slabs[0, PAD:].astype(f32)
    for d in range(1, PEERS):
        total = total + slabs[d, PAD:].astype(f32)
    if total.shape[0] == 32:
        lane = lax.broadcasted_iota(jnp.int32, (8, 128), 1)
        end = jnp.where(lane < 48, pltpu.roll(total[:8], 48, 1), pltpu.roll(total[8:16], 96, 1))
        total = jnp.concatenate([total, end], 0)
    elif total.shape[0] > 40:
        total = jnp.concatenate([total[i : i + 40] for i in range(0, total.shape[0], 40)], 1)
    lanes = total.shape[1]
    filled = jnp.concatenate([total, jnp.zeros((128 - 40, lanes), f32)], 0)
    grad_in[...] = filled.T[:size, :40]
    grad_out[...] = total[:, size : 2 * size]


def tables():
    lon = np.arange(NLON)
    freq = np.arange(NLON) % NF
    phase = (lon[:, None] * freq[None, :] % NLON) * (2.0 * math.pi / NLON)
    forward = np.where(np.arange(NLON)[None, :] >= NF, np.sin(phase), np.cos(phase))
    inverse = forward.T * (np.where(freq == 0, 1.0, 2.0) / NLON)[:, None]
    return jnp.asarray(forward.T, bf16), jnp.asarray(inverse.T, bf16)


def shape(*dims, dtype=bf16):
    return jax.ShapeDtypeStruct(dims, dtype)


VMEM = pl.BlockSpec(memory_space=pltpu.VMEM)
TOKEN = shape(8, 128, dtype=f32)
ANY = pl.BlockSpec(memory_space=pl.ANY)
SMEM = pl.BlockSpec(memory_space=pltpu.SMEM)


def call(kernel, out, ins, flops, moved, scratch=(), limit=24, **grid):
    options = dict(grid)
    if "grid" not in options:
        options["in_specs"] = ins
        options.setdefault("out_specs", jax.tree.map(lambda _: VMEM, out))
    return pl.pallas_call(
        kernel,
        out_shape=out,
        scratch_shapes=list(scratch),
        compiler_params=pltpu.CompilerParams(vmem_limit_bytes=limit << 20),
        cost_estimate=pl.CostEstimate(flops=int(flops), bytes_accessed=int(moved), transcendentals=0),
        **options,
    )


def body(mlp_input, out_cot, w_in, w_out, chan_weights, row_weights, basis_spectra, band_cols, band_widths):
    tokens_n = ROWS * LONS
    depth = lax.axis_size("z")
    n_lat = depth * lax.axis_size("core")
    part = 640 // n_lat
    lat, lon, core = lax.axis_index(LAT), lax.axis_index(LON), lax.axis_index("core")
    tokens = mlp_input.transpose(1, 0, 2).reshape(tokens_n, 640)
    cotangent = out_cot.transpose(1, 0, 2).reshape(tokens_n, 640)
    whole = lambda *dims: pl.BlockSpec(dims, lambda i: (0,) * len(dims))

    half = shape(depth, 2, part, 1280)
    half_spec = pl.BlockSpec((depth, 2, part, 640), lambda i: (0, 0, 0, i))
    pre_grad, mine, theirs = call(
        head_kernel,
        (pltpu.VMEM((tokens_n, 1280), bf16), pltpu.VMEM(half.shape, bf16), pltpu.VMEM(half.shape, bf16)),
        None,
        3e9,
        8e6,
        [pltpu.VMEM((640, tokens_n), bf16), pltpu.VMEM((640, tokens_n), bf16), pltpu.VMEM((2, 640, 640), f32)],
        limit=56,
        grid=(2,),
        in_specs=[
            SMEM,
            whole(tokens_n, 640),
            whole(tokens_n, 640),
            pl.BlockSpec((640, 640), lambda i: (0, i)),
            pl.BlockSpec((640, 640), lambda i: (i, 0)),
        ],
        out_specs=[pl.BlockSpec((tokens_n, 640), lambda i: (0, i)), half_spec, half_spec],
    )(core.reshape(1), tokens, cotangent, w_in, w_out)
    partner = lax.ppermute(theirs, "core", [(0, 1), (1, 0)])

    send = call(
        lift_kernel,
        pltpu.HBM((PEERS, PAD, 128), bf16),
        None,
        2e9,
        4e6,
        [pltpu.VMEM((TALL, 128), f32)],
        limit=48,
        grid=(1,),
        in_specs=[VMEM] * 3,
        out_specs=whole(PEERS, PAD, 128),
    )(pre_grad, cotangent, w_in)
    received = lax.all_to_all(send, LON, split_axis=0, concat_axis=0, tiled=True)

    mine, send = lax.optimization_barrier((mine, send))
    chip = (mine.astype(f32) + partner.astype(f32)).astype(bf16)
    column = lax.psum_scatter(chip, "z", scatter_dimension=0, tiled=True)

    own_mix, rim_mix, spread, ready = call(
        prep_kernel,
        (pltpu.HBM((GROUPS, NB * 128, 128), bf16), shape(NB * 256, 640), shape(NB, NLON, 128, dtype=f32), TOKEN),
        [SMEM] + [VMEM] * 5,
        1e9,
        6e6,
    )(
        jnp.stack([lat * ROWS, lon]).astype(jnp.int32),
        row_weights.transpose(0, 2, 1),
        band_cols.T,
        band_widths.reshape(1, -1),
        chan_weights,
        basis_spectra,
    )

    forward, inverse = tables()
    moved, first, last = call(
        open_kernel,
        (shape(NLON, 640), shape(NLON, 128), shape(NLON, 128)),
        [VMEM] * 2,
        1e8,
        2e6,
        [pltpu.VMEM((TALL, 128), f32)],
    )(received, ready)
    up = [(i, i + 1) for i in range(n_lat - 1)]
    before = lax.ppermute(last, LAT, up)
    after = lax.ppermute(first, LAT, [(b, a) for a, b in up])

    filtered = call(
        own_kernel,
        shape(NLON, 640, dtype=f32),
        [VMEM] * 3 + [ANY],
        8e8,
        5e6,
        [
            pltpu.VMEM((2, NLON, NB * 128), bf16),
            pltpu.VMEM((GROUPS, NB * 128, 128), bf16),
            pltpu.SemaphoreType.DMA((GROUPS,)),
        ],
    )(moved, forward, spread, pltpu.with_memory_space_constraint(own_mix, pltpu.HBM))

    extra = 32 if part == 40 else 40 * -(-2 * part // 128)
    answer = call(
        close_kernel,
        shape(PEERS, PAD + extra, 128),
        None,
        1.5e9,
        7e6,
        [pltpu.VMEM((NLON, NB * 256), bf16), pltpu.VMEM((TALL, 128), f32)],
        grid=(1,),
        in_specs=[VMEM] * 7,
        out_specs=whole(PEERS, PAD, 128),
    )(filtered, before, after, forward, inverse, spread, rim_mix)
    merged = call(
        merge_kernel,
        shape(PEERS, PAD + extra, 128),
        [ANY, VMEM],
        1e6,
        2e6,
        [pltpu.VMEM((PEERS, extra, 128), bf16), pltpu.SemaphoreType.DMA],
        out_specs=ANY,
        input_output_aliases={0: 0},
    )(answer, pltpu.with_memory_space_constraint(column, pltpu.HBM))
    returned = lax.all_to_all(merged, LON, split_axis=0, concat_axis=0, tiled=True)
    grid_grad, grad_in, grad_out = call(
        final_kernel,
        (shape(tokens_n, 640), shape(part, 40, dtype=f32), shape(40, part, dtype=f32)),
        [VMEM] * 2,
        1e8,
        2e6,
        [pltpu.VMEM((TALL, 128), f32)],
    )(returned, cotangent)
    grid_grad = grid_grad.reshape(LONS, ROWS, 640).transpose(1, 0, 2)
    return grid_grad, grad_in, grad_out


def solution(mesh):
    chips = Mesh(mesh.devices.reshape(-1, 2, 8, 4), ("z", "core", "y", "x"))
    grid = P(LAT, LON, None)
    return jax.shard_map(
        body,
        mesh=chips,
        in_specs=(grid, grid, P(), P(), P(), P(), P(), P(), P()),
        out_specs=(grid, P(LAT, LON), P(LON, LAT)),
        check_vma=False,
    )
```
